32 devices in a mesh: seq: 4 (over y, core), blk: 8 (over z, x).
Axes of the slice: x: 2, y: 2, z: 4, core: 2. Of those that a mesh axis runs over, the one named last changes fastest.
Arguments:
- hidden_states: bfloat16 [512, 4096], P('seq'), may hold values from -6 to 6
- query_weight: bfloat16 [4096, 4096], P('seq', 'blk')
- key_weight: bfloat16 [4096, 4096], P('seq', 'blk')
- value_weight: bfloat16 [4096, 4096], P('seq', 'blk'), may hold values from -0.09375 to 0.09375
- output_weight: bfloat16 [4096, 4096], P('blk', 'seq'), may hold values from -0.125 to 0.125
- query_gain: float32 [4096], P('blk'), may hold values from 0.7 to 3
- key_gain: float32 [4096], P('blk'), may hold values from 0.7 to 3
- attention_gain: float32 [4096], replicated, may hold values from 0.5 to 1.5
- gate_weight: bfloat16 [4096, 11008], P('seq', 'blk'), may hold values from -0.09375 to 0.09375
- up_weight: bfloat16 [4096, 11008], P('seq', 'blk'), may hold values from -0.09375 to 0.09375
- down_weight: bfloat16 [11008, 4096], P('blk', 'seq'), may hold values from -0.078125 to 0.078125
- feedforward_gain: float32 [4096], replicated, may hold values from 0.5 to 1.5
- cached_keys: bfloat16 [4, 1024, 4096], P('seq', None, 'blk'), may hold values from -6 to 6
- cached_values: bfloat16 [4, 1024, 4096], P('seq', None, 'blk'), may hold values from -6 to 6
- passage_order: int32 [4], replicated, may hold values from 0 to 3, each once
- separators: int32 [2, 2], replicated, may hold values from 1 to 64
- recompute_index: int32 [4, 96], replicated, may hold values from 0 to 1023, as said below
- prompt_lengths: int32 [2], replicated, may hold values from 16 to 64, as said below
Outputs:
- hidden_out: bfloat16 [512, 4096], P(('seq', 'blk'))
- blended_keys: bfloat16 [4, 1024, 4096], P('seq', None, 'blk')
- blended_values: bfloat16 [4, 1024, 4096], P('seq', None, 'blk')
The draws below stay inside these ranges and needn't reach their ends.
Inputs may be any that keep to these rules, and one draw needn't show every extreme that they name: `passage_order`: each passage id appears once. `recompute_index`: distinct within each passage. `prompt_lengths`: some request has all 64 of its new tokens live.
All inputs are finite; a program needn't handle non-finite values.
Results may differ from the reference program's by a relative error of at most 0.035.
Values may be sent and summed in bfloat16 or wider, within the bound.
A program may use at most 128 MiB of HBM per device.

```python
import math
import jax
import jax.numpy as jnp
from jax import lax

D = 4096
HEADS = 32
HD = 128
FF = 11008
PLEN = 1024
SEL = 96
PPR = 2
TOKN_DEV = 32
ROW_DEV = 128
ROWS = 512
PASSAGES = 4
REQS = 2
N_SEQ = 4
N_BLK = 8


def column_scales(key, columns):
    ramp = 3.0 ** (jnp.arange(columns, dtype=jnp.float32) / (columns - 1))
    rough = jax.random.uniform(key, (columns,), jnp.float32, 0.6, 1.6)
    return ramp * rough


def shared_noise(key):
    return jax.random.normal(jax.random.fold_in(key, 11), (D, HEADS * HD), jnp.float32)


def draw_key_weight(key, part):
    scales = column_scales(jax.random.fold_in(key, 12), HEADS * HD)
    return (shared_noise(key) * scales[None, :] * D ** (-0.5)).astype(jnp.bfloat16)


def draw_query_weight(key, part):
    noise = jax.random.normal(jax.random.fold_in(key, 21), (D, HEADS * HD), jnp.float32)
    scales = column_scales(jax.random.fold_in(key, 23), HEADS * HD)
    return (noise * scales[None, :] * D ** (-0.5)).astype(jnp.bfloat16)


def norm_gain(key):
    return jax.random.uniform(key, (HEADS * HD,), jnp.float32, 0.7, 1.4)


def draw_query_gain(key, part):
    return norm_gain(jax.random.fold_in(key, 31))


def draw_key_gain(key, part):
    return norm_gain(jax.random.fold_in(key, 32))


def draw_recompute_index(key, part):
    passage_keys = jax.random.split(jax.random.fold_in(key, 41), PASSAGES)

    def pick_rows(single_key):
        return jax.random.permutation(single_key, PLEN)[:SEL]
    return jax.vmap(pick_rows)(passage_keys).astype(jnp.int32)


def draw_prompt_lengths(key, part):
    longest = PPR * TOKN_DEV
    drawn = jax.random.randint(jax.random.fold_in(key, 51), (REQS,), longest // 4, longest + 1)
    chosen = jax.random.randint(jax.random.fold_in(key, 52), (), 0, REQS)
    return jnp.where(jnp.arange(REQS) == chosen, longest, drawn).astype(jnp.int32)


def touch_ends(result, rng, least, largest):
    index_at = [jax.random.randint(jax.random.fold_in(rng, axis), (), 0, length) for axis, length in enumerate(result.shape)]
    widest = result.shape.index(max(result.shape))
    neighbour = index_at[:widest] + [(index_at[widest] + 1) % result.shape[widest]] + index_at[widest + 1:]
    return result.at[tuple(index_at)].set(least).at[tuple(neighbour)].set(largest)


def strengthened(entries, key, source, target, shards_of, factor):
    owner, partner = [(jnp.arange(entries.shape[position]) // (entries.shape[position] // shards_of)).reshape([-1 if axis == position else 1 for axis in range(entries.ndim)]) for position in (source, target)]
    chosen = jax.random.permutation(key, shards_of)[partner]
    strong = (owner == chosen) | (owner == (partner + shards_of // 2) % shards_of)
    return jnp.where(strong, factor * entries, entries)


def level_of(stream_key, extent, shards, low, largest):
    level = 1.0
    for axis_at, shards_of in shards:
        heights = jax.random.uniform(jax.random.fold_in(jax.random.fold_in(stream_key, 6), axis_at), (shards_of,), jnp.float32, low / len(shards), largest / len(shards))
        level = level * jnp.repeat(jnp.exp(heights), extent[axis_at] // shards_of).reshape((-1,) + (1,) * (len(extent) - 1 - axis_at))
    return level


def centred(key, extent, spread, bound, shards=(), held_as=jnp.bfloat16):
    entries = spread * jax.random.normal(key, extent, jnp.float32)
    if shards:
        entries = entries * level_of(key, extent, shards, -0.22, 0.18)
    return jnp.clip(entries, -bound, bound).astype(held_as)


def heavy_noise(key, dims, scale, limit, cuts, heavy, kind=jnp.bfloat16):
    array = scale * jax.random.normal(key, dims, jnp.float32)
    if cuts:
        array = array * level_of(key, dims, cuts, -0.22, 0.18)
    return jnp.clip(strengthened(array, jax.random.fold_in(key, 3), *heavy), -limit, limit).astype(kind)


def setup_inputs(seed: int = 0) -> dict:
    key_list = jax.random.split(jax.random.key(seed), 19)
    return {
        "hidden_states": centred(key_list[0], (ROWS, D), 1.0, 6.0, ((0, 4),)),
        "query_weight": draw_query_weight(jax.random.fold_in(key_list[18], 71), 0),
        "key_weight": draw_key_weight(jax.random.fold_in(key_list[18], 71), 0),
        "value_weight": centred(key_list[3], (D, HEADS * HD), D ** -0.5, 0.09375, ((0, 4), (1, 8))),
        "output_weight": heavy_noise(key_list[4], (HEADS * HD, D), (HEADS * HD) ** -0.5, 0.125, ((0, 8), (1, 4)), (0, 1, 8, 2.0)),
        "query_gain": draw_query_gain(jax.random.fold_in(key_list[18], 71), 0),
        "key_gain": draw_key_gain(jax.random.fold_in(key_list[18], 71), 0),
        "attention_gain": jnp.clip(1.0 + 0.1 * jax.random.normal(key_list[7], (D,), jnp.float32), 0.5, 1.5),
        "gate_weight": centred(key_list[8], (D, FF), D ** -0.5, 0.09375, ((0, 4), (1, 8))),
        "up_weight": centred(key_list[9], (D, FF), D ** -0.5, 0.09375, ((0, 4), (1, 8))),
        "down_weight": heavy_noise(key_list[10], (FF, D), FF ** -0.5, 0.078125, ((0, 8), (1, 4)), (0, 1, 8, 2.0)),
        "feedforward_gain": jnp.clip(1.0 + 0.1 * jax.random.normal(key_list[11], (D,), jnp.float32), 0.5, 1.5),
        "cached_keys": centred(key_list[12], (PASSAGES, PLEN, HEADS * HD), 1.0, 6.0, ((0, 4), (2, 8))),
        "cached_values": centred(key_list[13], (PASSAGES, PLEN, HEADS * HD), 1.0, 6.0, ((0, 4), (2, 8))),
        "passage_order": jax.random.permutation(key_list[14], PASSAGES).astype(jnp.int32),
        "separators": touch_ends(jax.random.randint(key_list[15], (REQS, PPR), 1, 65), jax.random.fold_in(key_list[15], 1), 1, 64).astype(jnp.int32),
        "recompute_index": draw_recompute_index(jax.random.fold_in(key_list[18], 71), 0),
        "prompt_lengths": draw_prompt_lengths(jax.random.fold_in(key_list[18], 71), 0),
    }


EPSILON = 1e-06
ROPE_THETA = 500000.0
MASKED_SCORE = -1e+30

def frequencies():
    indices = jnp.arange(HD // 2, dtype=jnp.float32)
    return jnp.exp(indices * (-2.0 * math.log(ROPE_THETA) / HD))

def rotate(values, angles):
    half_width = values.shape[-1] // 2
    cosine = jnp.cos(angles)[:, None, :]
    sine = jnp.sin(angles)[:, None, :]
    first = values[..., :half_width]
    second = values[..., half_width:]
    return jnp.concatenate([first * cosine - second * sine, second * cosine + first * sine], axis=-1)

def normalize(matrix):
    return matrix * lax.rsqrt(lax.optimization_barrier(jnp.mean(matrix * matrix, axis=-1, keepdims=True)) + EPSILON)

def layout(passage_order, separators, recompute_index, prompt_lengths, seq_count):
    request_count = seq_count // PPR
    ordering = passage_order.reshape(request_count, PPR)
    slot_ids = jnp.arange(PPR, dtype=jnp.int32)
    opening = (slot_ids[None, :] * PLEN + jnp.cumsum(separators, axis=1)).astype(jnp.int32)
    flattened = ordering.reshape(-1)
    starts = jnp.zeros((seq_count,), jnp.int32).at[flattened].set(opening.reshape(-1))
    request_ids = jnp.repeat(jnp.arange(request_count, dtype=jnp.int32), PPR)
    owners = jnp.zeros((seq_count,), jnp.int32).at[flattened].set(request_ids)
    prompt_start = (opening[:, PPR - 1] + PLEN).astype(jnp.int32)
    devices = jnp.arange(seq_count, dtype=jnp.int32)
    new_request = (devices // PPR).astype(jnp.int32)
    new_index = ((devices % PPR)[:, None] * TOKN_DEV + jnp.arange(TOKN_DEV, dtype=jnp.int32)[None, :]).astype(jnp.int32)
    new_positions = (prompt_start[new_request][:, None] + new_index).astype(jnp.int32)
    new_live = new_index < prompt_lengths[new_request][:, None]
    picked_positions = (starts[:, None] + recompute_index).astype(jnp.int32)
    row_positions = jnp.concatenate([picked_positions, new_positions], axis=1).reshape(-1)
    row_live = jnp.concatenate([jnp.ones(picked_positions.shape, bool), new_live], axis=1).reshape(-1)
    return (starts, owners, new_request, new_positions, new_live, row_positions, row_live)

def grouped_sum(left, right, groups):
    inner = left.shape[1] // groups
    left_blocks = left.reshape(left.shape[0], groups, inner).transpose(1, 0, 2)
    right_blocks = right.reshape(groups, inner, right.shape[1])

    def add_block(carry, operands):
        term = jnp.dot(operands[0], operands[1], preferred_element_type=jnp.float32).astype(jnp.bfloat16)
        return (carry + lax.optimization_barrier(term).astype(jnp.float32), None)
    summed, unused = lax.scan(add_block, jnp.zeros((left.shape[0], right.shape[1]), jnp.float32), (left_blocks, right_blocks))
    return summed

def reference(hidden_states, query_weight, key_weight, value_weight, output_weight, query_gain, key_gain, attention_gain, gate_weight, up_weight, down_weight, feedforward_gain, cached_keys, cached_values, passage_order, separators, recompute_index, prompt_lengths):
    width = HEADS * HD
    starts, owners, new_request, new_positions, new_live, row_positions, row_live = layout(passage_order, separators, recompute_index, prompt_lengths, N_SEQ)
    frequency = frequencies()
    query_raw = jnp.dot(hidden_states, query_weight, preferred_element_type=jnp.float32)
    key_raw = jnp.dot(hidden_states, key_weight, preferred_element_type=jnp.float32)
    value_raw = jnp.dot(hidden_states, value_weight, preferred_element_type=jnp.float32)
    angles = row_positions.astype(jnp.float32)[:, None] * frequency[None, :]
    query_scaled = query_raw * lax.rsqrt(lax.optimization_barrier(jnp.mean(query_raw * query_raw, axis=1, keepdims=True)) + EPSILON) * query_gain
    key_scaled = key_raw * lax.rsqrt(lax.optimization_barrier(jnp.mean(key_raw * key_raw, axis=1, keepdims=True)) + EPSILON) * key_gain
    query = rotate(query_scaled.reshape(ROWS, HEADS, HD), angles).reshape(ROWS, width).astype(jnp.bfloat16)
    key_rows = rotate(key_scaled.reshape(ROWS, HEADS, HD), angles).reshape(ROWS, width).astype(jnp.bfloat16)
    value_rows = value_raw.astype(jnp.bfloat16)

    def shift_passage(passage_cache, passage_start):
        turned = jnp.broadcast_to(passage_start.astype(jnp.float32) * frequency, (PLEN, HD // 2))
        return rotate(passage_cache.astype(jnp.float32).reshape(PLEN, HEADS, HD), turned).reshape(PLEN, width).astype(jnp.bfloat16)
    moved = jax.vmap(shift_passage)(cached_keys, starts)
    passage_ids = jnp.arange(PASSAGES, dtype=jnp.int32)
    device_keys = key_rows.reshape(N_SEQ, ROW_DEV, width)
    device_values = value_rows.reshape(N_SEQ, ROW_DEV, width)
    blended_keys = moved.at[passage_ids[:, None], recompute_index].set(device_keys[:, :SEL])
    blended_values = cached_values.at[passage_ids[:, None], recompute_index].set(device_values[:, :SEL])
    all_keys = jnp.concatenate([blended_keys.reshape(PASSAGES * PLEN, width), device_keys[:, SEL:].reshape(-1, width)], axis=0)
    all_values = jnp.concatenate([blended_values.reshape(PASSAGES * PLEN, width), device_values[:, SEL:].reshape(-1, width)], axis=0)
    key_positions = jnp.concatenate([(starts[:, None] + jnp.arange(PLEN, dtype=jnp.int32)[None, :]).reshape(-1), new_positions.reshape(-1)])
    key_requests = jnp.concatenate([jnp.repeat(owners, PLEN), jnp.repeat(new_request, TOKN_DEV)])
    key_live = jnp.concatenate([jnp.ones((PASSAGES * PLEN,), bool), new_live.reshape(-1)])
    row_requests = jnp.concatenate([jnp.broadcast_to(owners[:, None], (N_SEQ, SEL)), jnp.broadcast_to(new_request[:, None], (N_SEQ, TOKN_DEV))], axis=1).reshape(-1)
    visible = (row_requests[:, None] == key_requests[None, :]) & (key_positions[None, :] <= row_positions[:, None]) & key_live[None, :]

    def one_head(operands):
        head_query, head_key, head_value = operands
        scores = jnp.dot(head_query, head_key.T, preferred_element_type=jnp.float32) * HD ** (-0.5)
        masked = jnp.where(visible, scores, MASKED_SCORE)
        peaks = lax.optimization_barrier(jnp.max(masked, axis=1, keepdims=True))
        exponentials = jnp.where(visible, jnp.exp(masked - peaks), 0.0)
        weighted = jnp.dot(exponentials.astype(jnp.bfloat16), head_value, preferred_element_type=jnp.float32)
        return weighted / lax.optimization_barrier(jnp.sum(exponentials, axis=1, keepdims=True))
    heads_first = lax.map(one_head, (query.reshape(ROWS, HEADS, HD).transpose(1, 0, 2), all_keys.reshape(-1, HEADS, HD).transpose(1, 0, 2), all_values.reshape(-1, HEADS, HD).transpose(1, 0, 2)))
    attention = heads_first.transpose(1, 0, 2).reshape(ROWS, width).astype(jnp.bfloat16)
    summed = grouped_sum(attention, output_weight, N_BLK)
    mixed = (hidden_states.astype(jnp.float32) + normalize(summed) * attention_gain).astype(jnp.bfloat16)
    gate_values = jnp.dot(mixed, gate_weight, preferred_element_type=jnp.float32)
    up_values = jnp.dot(mixed, up_weight, preferred_element_type=jnp.float32)
    activation = (jax.nn.silu(gate_values) * up_values).astype(jnp.bfloat16)
    feedforward = grouped_sum(activation, down_weight, N_BLK)
    hidden_out = (mixed.astype(jnp.float32) + normalize(feedforward) * feedforward_gain).astype(jnp.bfloat16)
    return (hidden_out, blended_keys, blended_values)
```

```python
import functools
import math

import jax
import jax.numpy as jnp
from jax import lax
from jax.experimental import pallas as pl
from jax.experimental.pallas import tpu as pltpu
from jax.sharding import PartitionSpec as P

HD = 128
PLEN = 1024
SEL = 96
PPR = 2
TOKN_DEV = 32

EPSILON = 1e-06
ROPE_THETA = 500000.0
MASKED_SCORE = -1e30
MESH = pl.DeviceIdType.MESH
ANY = pl.BlockSpec(memory_space=pl.ANY)
VMEM = pl.BlockSpec(memory_space=pltpu.VMEM)


def greet(peers):
    barrier = pltpu.get_barrier_semaphore()
    for peer in peers:
        pl.semaphore_signal(barrier, inc=1, device_id=peer, device_id_type=MESH)
    pl.semaphore_wait(barrier, len(peers))


def peers_of(axis, count):
    me = lax.axis_index(axis)
    return [{axis: lax.rem(me + offset, count)} for offset in range(1, count)]


def send(source, target, send_sem, recv_sem, peer):
    copy = pltpu.make_async_remote_copy(
        src_ref=source,
        dst_ref=target,
        send_sem=send_sem,
        recv_sem=recv_sem,
        device_id=peer,
        device_id_type=MESH,
    )
    copy.start()
    return copy


def exchange_kernel(axis, count, array_count, scatter, *refs):
    sources, targets = refs[:array_count], refs[array_count : 2 * array_count]
    send_sems, recv_sems, local_sems = refs[2 * array_count :]
    me = lax.axis_index(axis)
    peers = peers_of(axis, count)
    greet(peers)
    copies = []
    for offset in range(1, count):
        for k in range(array_count):
            peer = peers[offset - 1]
            source = sources[k].at[peer[axis]] if scatter else sources[k]
            copies.append(
                send(
                    source,
                    targets[k].at[me],
                    send_sems.at[k, offset],
                    recv_sems.at[k, offset],
                    peer,
                )
            )
    for k in range(array_count):
        source = sources[k].at[me] if scatter else sources[k]
        copy = pltpu.make_async_copy(source, targets[k].at[me], local_sems.at[k])
        copy.start()
        copies.append(copy)
    for copy in copies:
        copy.wait()


def exchange(axis, arrays, scatter, collective_id):
    count = lax.axis_size(axis)
    shapes = [
        jax.ShapeDtypeStruct(a.shape if scatter else (count,) + a.shape, a.dtype) for a in arrays
    ]
    return pl.pallas_call(
        functools.partial(exchange_kernel, axis, count, len(arrays), scatter),
        out_shape=shapes,
        in_specs=[ANY] * len(arrays),
        out_specs=[ANY] * len(arrays),
        scratch_shapes=[
            pltpu.SemaphoreType.DMA((len(arrays), count)),
            pltpu.SemaphoreType.DMA((len(arrays), count)),
            pltpu.SemaphoreType.DMA((len(arrays),)),
        ],
        compiler_params=pltpu.CompilerParams(collective_id=collective_id, has_side_effects=True),
    )(*arrays)


def gather_kernel(
    axis,
    count,
    sum_axis,
    sum_count,
    data_ref,
    squares_ref,
    gathered_ref,
    sums_ref,
    landing,
    data_send,
    data_recv,
    part_send,
    part_recv,
    sum_send,
    sum_recv,
    local_sem,
):
    me = lax.axis_index(axis)
    peers = peers_of(axis, count)
    sum_peers = peers_of(sum_axis, sum_count)
    greet(peers + sum_peers)
    parts = [
        send(
            squares_ref,
            landing.at[offset],
            part_send.at[offset],
            part_recv.at[offset],
            sum_peers[offset - 1],
        )
        for offset in range(1, sum_count)
    ]
    copies = [
        send(
            data_ref,
            gathered_ref.at[me],
            data_send.at[offset],
            data_recv.at[offset],
            peers[offset - 1],
        )
        for offset in range(1, count)
    ]
    local = pltpu.make_async_copy(data_ref, gathered_ref.at[me], local_sem)
    local.start()
    total = squares_ref[...]
    for offset in range(1, sum_count):
        parts[offset - 1].wait()
        total += landing[offset]
    sums_ref[me] = total
    for offset in range(1, count):
        copies.append(
            send(
                sums_ref.at[me],
                sums_ref.at[me],
                sum_send.at[offset],
                sum_recv.at[offset],
                peers[offset - 1],
            )
        )
    for copy in copies:
        copy.wait()
    local.wait()


def gather_with_sums(data, squares, axis, sum_axis, collective_id):
    count, sum_count = lax.axis_size(axis), lax.axis_size(sum_axis)
    return pl.pallas_call(
        functools.partial(gather_kernel, axis, count, sum_axis, sum_count),
        out_shape=[
            jax.ShapeDtypeStruct((count,) + data.shape, data.dtype),
            jax.ShapeDtypeStruct((count,) + squares.shape, squares.dtype),
        ],
        in_specs=[ANY, VMEM],
        out_specs=[ANY, VMEM],
        scratch_shapes=[
            pltpu.VMEM((sum_count,) + squares.shape, squares.dtype),
            pltpu.SemaphoreType.DMA((count,)),
            pltpu.SemaphoreType.DMA((count,)),
            pltpu.SemaphoreType.DMA((sum_count,)),
            pltpu.SemaphoreType.DMA((sum_count,)),
            pltpu.SemaphoreType.DMA((count,)),
            pltpu.SemaphoreType.DMA((count,)),
            pltpu.SemaphoreType.DMA,
        ],
        compiler_params=pltpu.CompilerParams(collective_id=collective_id, has_side_effects=True),
    )(data, squares)


def attention_kernel(
    query_ref,
    factor_ref,
    old_limit_ref,
    new_limit_ref,
    picked_ref,
    turn_ref,
    old_keys_ref,
    old_values_ref,
    key_rows_ref,
    value_rows_ref,
    keys_ref,
    values_ref,
    weighted_ref,
    stats_ref,
):
    @pl.when(pl.program_id(1) == 0)
    def blend():
        row_count = key_rows_ref.shape[0]
        token = lax.broadcasted_iota(jnp.int32, (PLEN, row_count), 0)
        hit = token == picked_ref[...]
        chosen = jnp.where(hit, 1.0, 0.0)
        replaced = jnp.max(chosen, axis=1, keepdims=True) > 0.5
        chosen = chosen.astype(jnp.bfloat16)
        old = old_keys_ref[...].astype(jnp.float32)
        turned = old * turn_ref[0:1, :] + pltpu.roll(old, HD // 2, 1) * turn_ref[1:2, :]
        new_keys = jnp.dot(chosen, key_rows_ref[...], preferred_element_type=jnp.float32)
        keys_ref[...] = jnp.where(replaced, new_keys, turned).astype(jnp.bfloat16)
        new_values = jnp.dot(chosen, value_rows_ref[...], preferred_element_type=jnp.float32)
        values_ref[...] = jnp.where(
            replaced, new_values, old_values_ref[...].astype(jnp.float32)
        ).astype(jnp.bfloat16)

    query = (query_ref[...].astype(jnp.float32) * factor_ref[...]).astype(jnp.bfloat16)
    contract = (((1,), (1,)), ((), ()))
    old_scores = lax.dot_general(
        query, keys_ref[...], contract, preferred_element_type=jnp.float32
    )
    new_scores = lax.dot_general(
        query, key_rows_ref[...], contract, preferred_element_type=jnp.float32
    )
    scale = HD ** (-0.5)
    old_seen = lax.broadcasted_iota(jnp.int32, old_scores.shape, 1) <= old_limit_ref[...]
    new_token = lax.broadcasted_iota(jnp.int32, new_scores.shape, 1) - SEL
    new_seen = (new_token >= 0) & (new_token <= new_limit_ref[...])
    old_scores = jnp.where(old_seen, old_scores * scale, MASKED_SCORE)
    new_scores = jnp.where(new_seen, new_scores * scale, MASKED_SCORE)
    peak = jnp.maximum(
        jnp.max(old_scores, axis=1, keepdims=True), jnp.max(new_scores, axis=1, keepdims=True)
    )
    old_weights = jnp.where(old_seen, jnp.exp(old_scores - peak), 0.0)
    new_weights = jnp.where(new_seen, jnp.exp(new_scores - peak), 0.0)
    total = jnp.sum(old_weights, axis=1, keepdims=True) + jnp.sum(
        new_weights, axis=1, keepdims=True
    )
    weighted = jnp.dot(
        old_weights.astype(jnp.bfloat16), values_ref[...], preferred_element_type=jnp.float32
    ) + jnp.dot(
        new_weights.astype(jnp.bfloat16), value_rows_ref[...], preferred_element_type=jnp.float32
    )
    weighted_ref[...] = weighted.astype(jnp.bfloat16)
    lane = lax.broadcasted_iota(jnp.int32, weighted.shape, 1)
    stats = jnp.transpose(jnp.where(lane == 0, peak, total))
    stats_ref[0] = stats[:8, :]


def attend(
    queries, factor, old_limit, new_limit, picked, turn, old_keys, old_values, key_rows, value_rows
):
    total_rows, width = queries.shape
    row_count = key_rows.shape[0]
    head_count = width // HD
    block = min(total_rows, 512)
    by_row = pl.BlockSpec((block, 1), lambda h, i: (i, 0))
    by_head = pl.BlockSpec((PLEN, HD), lambda h, i: (0, h))
    rows_by_head = pl.BlockSpec((row_count, HD), lambda h, i: (0, h))
    tile = pl.BlockSpec((block, HD), lambda h, i: (i, h))
    return pl.pallas_call(
        attention_kernel,
        grid=(head_count, total_rows // block),
        out_shape=[
            jax.ShapeDtypeStruct((PLEN, width), jnp.bfloat16),
            jax.ShapeDtypeStruct((PLEN, width), jnp.bfloat16),
            jax.ShapeDtypeStruct((total_rows, width), jnp.bfloat16),
            jax.ShapeDtypeStruct((head_count, 8, total_rows), jnp.float32),
        ],
        in_specs=[
            tile,
            by_row,
            by_row,
            by_row,
            pl.BlockSpec((1, row_count), lambda h, i: (0, 0)),
            pl.BlockSpec((8, HD), lambda h, i: (0, 0)),
            by_head,
            by_head,
            rows_by_head,
            rows_by_head,
        ],
        out_specs=[
            by_head,
            by_head,
            tile,
            pl.BlockSpec((1, 8, block), lambda h, i: (h, 0, i)),
        ],
        compiler_params=pltpu.CompilerParams(vmem_limit_bytes=48 * 1024 * 1024),
    )(
        queries,
        factor,
        old_limit,
        new_limit,
        picked,
        turn,
        old_keys,
        old_values,
        key_rows,
        value_rows,
    )


def frequencies():
    indices = jnp.arange(HD // 2, dtype=jnp.float32)
    return jnp.exp(indices * (-2.0 * math.log(ROPE_THETA) / HD))


def rotate(values, angles):
    half_width = values.shape[-1] // 2
    cosine = jnp.cos(angles)[:, None, :]
    sine = jnp.sin(angles)[:, None, :]
    first = values[..., :half_width]
    second = values[..., half_width:]
    return jnp.concatenate(
        [first * cosine - second * sine, second * cosine + first * sine], axis=-1
    )


def layout(passage_order, separators, recompute_index, seq_count):
    devices = jnp.arange(seq_count, dtype=jnp.int32)
    slots = jnp.arange(PPR, dtype=jnp.int32)
    earlier = slots[None, :, None] >= slots[None, None, :]
    opening = slots[None, :] * PLEN + jnp.sum(
        jnp.where(earlier, separators[:, None, :], 0), axis=2
    )
    hit = passage_order[None, :] == devices[:, None]
    starts = jnp.sum(jnp.where(hit, opening.reshape(-1)[None, :], 0), axis=1)
    owners = jnp.sum(jnp.where(hit, (devices // PPR)[None, :], 0), axis=1)
    prompt_start = jnp.repeat(opening[:, PPR - 1] + PLEN, PPR)
    offsets = (devices % PPR) * TOKN_DEV
    new_starts = prompt_start + offsets
    new_positions = new_starts[:, None] + jnp.arange(TOKN_DEV, dtype=jnp.int32)[None, :]
    positions = jnp.concatenate([starts[:, None] + recompute_index, new_positions], axis=1)
    requests = jnp.concatenate(
        [
            jnp.broadcast_to(owners[:, None], recompute_index.shape),
            jnp.broadcast_to((devices // PPR)[:, None], new_positions.shape),
        ],
        axis=1,
    )
    return starts, owners, new_starts, offsets, positions, requests


def total_of(parts):
    return jnp.sum(parts.astype(jnp.float32), axis=0)


def shards(
    hidden_states,
    query_weight,
    key_weight,
    value_weight,
    output_weight,
    query_gain,
    key_gain,
    attention_gain,
    gate_weight,
    up_weight,
    down_weight,
    feedforward_gain,
    cached_keys,
    cached_values,
    passage_order,
    separators,
    recompute_index,
    prompt_lengths,
):
    seq_count = lax.axis_size("seq")
    blk_count = lax.axis_size("blk")
    seq_index = lax.axis_index("seq")
    blk_index = lax.axis_index("blk")
    row_count, model_width = hidden_states.shape
    depth, local_width = query_weight.shape
    head_count = local_width // HD
    total_rows = row_count * seq_count
    part_rows = row_count // blk_count
    full_width = local_width * blk_count

    def mine(array):
        return lax.dynamic_index_in_dim(array, seq_index, 0, keepdims=False)

    starts, owners, new_starts, offsets, positions, requests = layout(
        passage_order, separators, recompute_index, seq_count
    )
    frequency = frequencies()
    passage_start = mine(starts)
    own_request = seq_index // PPR
    old_limit = jnp.where(requests == mine(owners), positions - passage_start, -1)
    live_limit = lax.dynamic_index_in_dim(prompt_lengths, own_request, 0, False) - 1 - mine(offsets)
    new_limit = jnp.where(
        requests == own_request, jnp.minimum(positions - mine(new_starts), live_limit), -1
    )
    picked = jnp.concatenate(
        [mine(recompute_index), jnp.full((row_count - SEL,), -1, jnp.int32)]
    ).reshape(1, row_count)
    turn_angles = passage_start.astype(jnp.float32) * frequency
    turn_cosine, turn_sine = jnp.cos(turn_angles), jnp.sin(turn_angles)
    turn = jnp.concatenate(
        [
            jnp.concatenate([turn_cosine, turn_cosine])[None],
            jnp.concatenate([-turn_sine, turn_sine])[None],
            jnp.zeros((6, HD), jnp.float32),
        ]
    )
    angles = mine(positions).astype(jnp.float32)[:, None] * frequency[None, :]

    columns = hidden_states.reshape(row_count, seq_count, depth).transpose(1, 0, 2)
    (hidden,) = exchange("seq", [columns], True, 0)
    hidden = hidden.reshape(total_rows, depth)

    def partial(rows, weight):
        product = jnp.dot(rows, weight, preferred_element_type=jnp.float32)
        return product.astype(jnp.bfloat16).reshape(seq_count, row_count, weight.shape[1])

    query_raw, key_raw, value_raw = (
        total_of(parts)
        for parts in exchange(
            "seq",
            [
                partial(hidden, query_weight),
                partial(hidden, key_weight),
                partial(hidden, value_weight),
            ],
            True,
            1,
        )
    )
    squares = jnp.concatenate(
        [
            jnp.sum(query_raw * query_raw, axis=1)[None],
            jnp.sum(key_raw * key_raw, axis=1)[None],
            jnp.zeros((6, row_count), jnp.float32),
        ]
    )

    def turned(raw, gain):
        return rotate((raw * gain).reshape(row_count, head_count, HD), angles).reshape(
            row_count, local_width
        )

    queries, sums = gather_with_sums(
        turned(query_raw, query_gain).astype(jnp.bfloat16), squares, "seq", "blk", 2
    )
    factors = lax.rsqrt(sums[:, :2] / full_width + EPSILON)
    key_rows = (turned(key_raw, key_gain) * mine(factors)[1][:, None]).astype(jnp.bfloat16)
    value_rows = value_raw.astype(jnp.bfloat16)
    passage_keys, passage_values, weighted, stats = attend(
        queries.reshape(total_rows, local_width),
        factors[:, 0].reshape(total_rows, 1),
        old_limit.reshape(total_rows, 1),
        new_limit.reshape(total_rows, 1),
        picked,
        turn,
        cached_keys[0],
        cached_values[0],
        key_rows,
        value_rows,
    )
    stats = (
        stats[:, :2]
        .reshape(head_count, 2, seq_count, row_count)
        .transpose(2, 1, 0, 3)
        .reshape(seq_count, 2 * head_count, row_count)
    )
    weighted, stats = exchange(
        "seq", [weighted.reshape(seq_count, row_count, local_width), stats], True, 3
    )
    peaks, totals = stats[:, :head_count], stats[:, head_count:]
    shares = jnp.exp(peaks - jnp.max(peaks, axis=0))
    shares = shares / jnp.sum(shares * totals, axis=0)
    shares = shares.transpose(0, 2, 1)[..., None]
    attention = (
        jnp.sum(
            weighted.astype(jnp.float32).reshape(seq_count, row_count, head_count, HD) * shares,
            axis=0,
        )
        .reshape(row_count, local_width)
        .astype(jnp.bfloat16)
    )
    (attention,) = exchange("seq", [attention], False, 4)

    def by_block(rows):
        return rows.reshape(seq_count, blk_count, part_rows, depth).transpose(1, 0, 2, 3)

    projected = jnp.dot(
        attention.reshape(total_rows, local_width),
        output_weight,
        preferred_element_type=jnp.float32,
    ).astype(jnp.bfloat16)
    (summed,) = exchange("blk", [by_block(projected)], True, 5)
    summed = total_of(summed)
    summed_squares = jnp.sum(summed * summed, axis=2).reshape(1, -1)
    summed_squares = jnp.pad(
        summed_squares, ((0, 7), (0, -summed_squares.shape[1] % 128))
    )
    summed, sums = gather_with_sums(
        summed.astype(jnp.bfloat16), summed_squares, "blk", "seq", 6
    )
    sums = sums[:, 0, : seq_count * part_rows].reshape(blk_count, seq_count, part_rows)
    factors = lax.rsqrt(sums / model_width + EPSILON)
    my_gain = lax.dynamic_slice_in_dim(attention_gain, seq_index * depth, depth)
    update = (summed.astype(jnp.float32) * factors[..., None] * my_gain).transpose(1, 0, 2, 3)
    mixed = (
        hidden.reshape(seq_count, blk_count, part_rows, depth).astype(jnp.float32) + update
    ).astype(jnp.bfloat16)
    mixed_rows = mixed.reshape(total_rows, depth)
    gate_values, up_values = (
        total_of(parts)
        for parts in exchange(
            "seq", [partial(mixed_rows, gate_weight), partial(mixed_rows, up_weight)], True, 7
        )
    )
    activation = (jax.nn.silu(gate_values) * up_values).astype(jnp.bfloat16)
    (activation,) = exchange("seq", [activation], False, 8)
    product = jnp.dot(
        activation.reshape(total_rows, -1), down_weight, preferred_element_type=jnp.float32
    ).astype(jnp.bfloat16)
    (feedforward,) = exchange("blk", [by_block(product)], True, 9)
    feedforward = total_of(feedforward).astype(jnp.bfloat16)
    my_mixed = lax.dynamic_index_in_dim(mixed, blk_index, 1, keepdims=False)
    feedforward, my_mixed = exchange("seq", [feedforward, my_mixed], True, 10)

    def whole(parts):
        return parts.astype(jnp.float32).transpose(1, 0, 2).reshape(part_rows, model_width)

    feedforward = whole(feedforward)
    normalized = feedforward * lax.rsqrt(
        jnp.mean(feedforward * feedforward, axis=-1, keepdims=True) + EPSILON
    )
    hidden_out = (whole(my_mixed) + normalized * feedforward_gain).astype(jnp.bfloat16)
    return (hidden_out, passage_keys[None], passage_values[None])


def solution(mesh):
    return jax.shard_map(
        shards,
        mesh=mesh,
        in_specs=(
            P("seq", None),
            P("seq", "blk"),
            P("seq", "blk"),
            P("seq", "blk"),
            P("blk", "seq"),
            P("blk"),
            P("blk"),
            P(),
            P("seq", "blk"),
            P("seq", "blk"),
            P("blk", "seq"),
            P(),
            P("seq", None, "blk"),
            P("seq", None, "blk"),
            P(),
            P(),
            P(),
            P(),
        ),
        out_specs=(P(("seq", "blk"), None), P("seq", None, "blk"), P("seq", None, "blk")),
        check_vma=False,
    )
```

```python
import functools
import math

import jax
import jax.numpy as jnp
from jax import lax
from jax.experimental import pallas as pl
from jax.experimental.pallas import tpu as pltpu
from jax.sharding import PartitionSpec as P

HD = 128
PLEN = 1024
SEL = 96
PPR = 2
TOKN_DEV = 32

EPSILON = 1e-06
ROPE_THETA = 500000.0
MASKED_SCORE = -1e30
MESH = pl.DeviceIdType.MESH
ANY = pl.BlockSpec(memory_space=pl.ANY)
VMEM = pl.BlockSpec(memory_space=pltpu.VMEM)


def greet(peers):
    barrier = pltpu.get_barrier_semaphore()
    for peer in peers:
        pl.semaphore_signal(barrier, inc=1, device_id=peer, device_id_type=MESH)
    pl.semaphore_wait(barrier, len(peers))


class Links:
    def __init__(self, send_sems, recv_sems, local_sems):
        self.send_sems, self.recv_sems, self.local_sems = send_sems, recv_sems, local_sems
        self.sent, self.moved = 0, 0
        self.unsent, self.started = [], []

    def send(self, source, target, peer):
        copy = pltpu.make_async_remote_copy(
            src_ref=source,
            dst_ref=target,
            send_sem=self.send_sems.at[self.sent],
            recv_sem=self.recv_sems.at[self.sent],
            device_id=peer,
            device_id_type=MESH,
        )
        copy.start()
        self.sent += 1
        self.unsent.append(copy)
        return copy

    def move(self, source, target):
        copy = pltpu.make_async_copy(source, target, self.local_sems.at[self.moved])
        copy.start()
        self.moved += 1
        return copy

    def finish(self):
        for copy in self.unsent:
            copy.wait_send()


class Pairs:
    def __init__(self, count):
        self.count, self.pairs = count, count // 2
        self.me = lax.axis_index("seq")
        self.pair, self.core = lax.div(self.me, 2), lax.rem(self.me, 2)

    def index(self, offset, other):
        core = 1 - self.core if other else self.core
        return lax.rem(self.pair + offset, self.pairs) * 2 + core

    def peer(self, offset, other):
        return {"seq": self.index(offset, other)}

    def everyone(self):
        return [
            (offset, other)
            for offset in list(range(1, self.pairs)) + [0]
            for other in (1, 0)
            if offset or other
        ]

    def source(self, offset, other):
        return ((self.pairs - offset) % self.pairs, other)


class Grid:
    def __init__(self, count):
        self.width = grid_width(count)
        self.depth = count // self.width
        self.me = lax.axis_index("blk")
        self.z, self.x = lax.div(self.me, self.width), lax.rem(self.me, self.width)

    def along_x(self, offset):
        return lax.rem(self.x + offset, self.width)

    def along_z(self, offset):
        return lax.rem(self.z + offset, self.depth)

    def x_peer(self, offset):
        return {"blk": self.z * self.width + self.along_x(offset)}

    def z_peer(self, offset):
        return {"blk": self.along_z(offset) * self.width + self.x}

    def neighbours(self):
        return [self.x_peer(o) for o in range(1, self.width)] + [
            self.z_peer(o) for o in range(1, self.depth)
        ]


def grid_width(count):
    width = 1
    while 8 * width * width <= count:
        width *= 2
    return width


def reduce_over_seq(links, seq, partial, outgoing, from_sibling, from_pairs):
    near, far = {}, []
    order = list(range(1, seq.pairs)) + [0]
    for offset in order:
        for k, piece in enumerate(partial(offset, 1)):
            outgoing[offset, 0, k] = piece.astype(jnp.bfloat16)
        near[offset] = links.send(
            outgoing.at[offset, 0], from_sibling.at[offset], seq.peer(0, 1)
        )
    for offset in order[:-1]:
        pieces = partial(offset, 0)
        near[offset].wait_recv()
        for k, piece in enumerate(pieces):
            outgoing[offset, 1, k] = (piece + from_sibling[offset, k].astype(jnp.float32)).astype(
                jnp.bfloat16
            )
        far.append(
            links.send(outgoing.at[offset, 1], from_pairs.at[offset], seq.peer(offset, 0))
        )
    totals = list(partial(0, 0))
    near[0].wait_recv()
    totals = [t + from_sibling[0, k].astype(jnp.float32) for k, t in enumerate(totals)]
    for offset, copy in zip(order[:-1], far):
        copy.wait_recv()
        totals = [t + from_pairs[offset, k].astype(jnp.float32) for k, t in enumerate(totals)]
    return totals


def share_over_seq(links, seq, buffer, use):
    mine = buffer.at[seq.me]
    far = {o: links.send(mine, mine, seq.peer(o, 0)) for o in range(1, seq.pairs)}
    near = {0: links.send(mine, mine, seq.peer(0, 1))}
    use(seq.me)
    near[0].wait_recv()
    use(seq.index(0, 1))
    for offset in range(1, seq.pairs):
        far[seq.pairs - offset].wait_recv()
        block = buffer.at[seq.index(offset, 0)]
        near[offset] = links.send(block, block, seq.peer(0, 1))
        use(seq.index(offset, 0))
    for offset in range(1, seq.pairs):
        near[offset].wait_recv()
        use(seq.index(offset, 1))


class BlockSum:
    def __init__(self, links, grid, seq, parts, from_x, summed, from_z):
        self.links, self.grid, self.seq = links, grid, seq
        self.parts, self.from_x, self.summed, self.from_z = parts, from_x, summed, from_z
        self.order, self.x_copies, self.z_copies = [], [], []

    def put(self, s, product):
        grid = self.grid
        rows = self.parts.shape[3]
        for z in range(grid.depth):
            for x in range(grid.width):
                at = (z * grid.width + x) * rows
                self.parts[s, z, x] = product[at : at + rows].astype(jnp.bfloat16)
        step = len(self.order)
        self.order.append(s)
        self.x_copies.append(
            [
                self.links.send(
                    self.parts.at[s, :, grid.along_x(o)],
                    self.from_x.at[o, step],
                    grid.x_peer(o),
                )
                for o in range(1, grid.width)
            ]
        )
        if step:
            self.pass_on(step - 1)

    def pass_on(self, step):
        grid = self.grid
        s = self.order[step]
        total = self.parts[s, :, grid.x].astype(jnp.float32)
        for o, copy in enumerate(self.x_copies[step], 1):
            copy.wait_recv()
            total += self.from_x[o, step].astype(jnp.float32)
        self.summed[step] = total.astype(jnp.bfloat16)
        self.z_copies.append(
            [
                self.links.send(
                    self.summed.at[step, grid.along_z(o)],
                    self.from_z.at[o, step],
                    grid.z_peer(o),
                )
                for o in range(1, grid.depth)
            ]
        )

    def totals(self):
        self.pass_on(len(self.order) - 1)
        for step, s in enumerate(self.order):
            total = self.summed[step, self.grid.z].astype(jnp.float32)
            for o, copy in enumerate(self.z_copies[step], 1):
                copy.wait_recv()
                total += self.from_z[o, step].astype(jnp.float32)
            yield s, total


def block_sum_scratch(seq_count, blk_count, part_rows, depth):
    width = grid_width(blk_count)
    height = blk_count // width
    return [
        pltpu.VMEM((seq_count, height, width, part_rows, depth), jnp.bfloat16),
        pltpu.VMEM((width, seq_count, height, part_rows, depth), jnp.bfloat16),
        pltpu.VMEM((seq_count, height, part_rows, depth), jnp.bfloat16),
        pltpu.VMEM((height, seq_count, part_rows, depth), jnp.bfloat16),
    ]


def semaphores(copies):
    return [
        pltpu.SemaphoreType.DMA((copies,)),
        pltpu.SemaphoreType.DMA((copies,)),
        pltpu.SemaphoreType.DMA((8,)),
    ]


def params(collective_id):
    return pltpu.CompilerParams(
        collective_id=collective_id,
        has_side_effects=True,
        vmem_limit_bytes=48 * 1024 * 1024,
    )


def columns_of(rows):
    lanes = rows.shape[1]
    return jnp.transpose(
        jnp.concatenate([rows, jnp.zeros((lanes - rows.shape[0], lanes), jnp.float32)])
    )


def project_kernel(
    seq_count,
    blk_count,
    states_ref,
    query_weight,
    key_weight,
    value_weight,
    query_gain,
    key_gain,
    cosine_ref,
    sine_ref,
    hidden_ref,
    queries_ref,
    factors_ref,
    key_rows_ref,
    value_rows_ref,
    outgoing,
    from_sibling,
    from_pairs,
    weights,
    squares,
    landing,
    sums,
    *sems,
):
    seq = Pairs(seq_count)
    row_count, depth = hidden_ref.shape[1:]
    width = key_rows_ref.shape[1]
    links = Links(*sems)
    blk = lax.axis_index("blk")
    blk_peers = [{"blk": lax.rem(blk + o, blk_count)} for o in range(1, blk_count)]
    loads = [
        links.move(ref, weights.at[k])
        for k, ref in enumerate((query_weight, key_weight, value_weight))
    ]
    own = links.move(
        states_ref.at[:, pl.ds(pl.multiple_of(seq.me * depth, depth), depth)],
        hidden_ref.at[seq.me],
    )
    greet([seq.peer(*which) for which in seq.everyone()] + blk_peers)
    arrivals = {}
    for which in seq.everyone():
        column = pl.multiple_of(seq.index(*which) * depth, depth)
        arrivals[which] = links.send(
            states_ref.at[:, pl.ds(column, depth)], hidden_ref.at[seq.me], seq.peer(*which)
        )
    for load in loads:
        load.wait()

    def partial(offset, other):
        if offset or other:
            arrivals[seq.source(offset, other)].wait_recv()
        else:
            own.wait()
        rows = hidden_ref[seq.index(offset, other)]
        return [
            jnp.dot(rows, weights[k], preferred_element_type=jnp.float32) for k in range(3)
        ]

    query, key, value = reduce_over_seq(links, seq, partial, outgoing, from_sibling, from_pairs)
    value_rows_ref[...] = value.astype(jnp.bfloat16)
    lane = lax.broadcasted_iota(jnp.int32, (row_count, HD), 1)
    query_squares = jnp.sum(query * query, axis=1, keepdims=True)
    key_squares = jnp.sum(key * key, axis=1, keepdims=True)
    squares[...] = jnp.transpose(jnp.where(lane == 0, query_squares, key_squares))[:8]
    parts = [
        links.send(squares, landing.at[o], blk_peers[o - 1]) for o in range(1, blk_count)
    ]

    def turned(raw, gain, h):
        piece = raw[:, h * HD : (h + 1) * HD] * gain[:, h * HD : (h + 1) * HD]
        return piece * cosine_ref[...] + pltpu.roll(piece, HD // 2, 1) * sine_ref[...]

    for h in range(width // HD):
        queries_ref[seq.me, :, h * HD : (h + 1) * HD] = turned(query, query_gain, h).astype(
            jnp.bfloat16
        )
    mine = queries_ref.at[seq.me]
    far = {o: links.send(mine, mine, seq.peer(o, 0)) for o in range(1, seq.pairs)}
    near = [links.send(mine, mine, seq.peer(0, 1))]
    total = squares[...]
    for o, copy in enumerate(parts, 1):
        copy.wait_recv()
        total += landing[o]
    sums[seq.me] = total
    sum_copies = [
        links.send(sums.at[seq.me], sums.at[seq.me], seq.peer(*which))
        for which in seq.everyone()
    ]
    key_factor = lax.rsqrt(columns_of(total) / (width * blk_count) + EPSILON)[:, 1:2]
    for h in range(width // HD):
        key_rows_ref[:, h * HD : (h + 1) * HD] = (turned(key, key_gain, h) * key_factor).astype(
            jnp.bfloat16
        )
    for offset in range(1, seq.pairs):
        far[seq.pairs - offset].wait_recv()
        block = queries_ref.at[seq.index(offset, 0)]
        near.append(links.send(block, block, seq.peer(0, 1)))
    for copy in sum_copies + near:
        copy.wait_recv()
    for d in range(seq_count):
        factors_ref[d] = lax.rsqrt(columns_of(sums[d]) / (width * blk_count) + EPSILON)[:, 0:1]
    links.finish()


def project(states, weights, gains, cosine, sine, seq_count, blk_count):
    row_count = states.shape[0]
    depth, width = weights[0].shape
    pairs = seq_count // 2
    bf16, f32 = jnp.bfloat16, jnp.float32
    return pl.pallas_call(
        functools.partial(project_kernel, seq_count, blk_count),
        out_shape=[
            jax.ShapeDtypeStruct((seq_count, row_count, depth), bf16),
            jax.ShapeDtypeStruct((seq_count, row_count, width), bf16),
            jax.ShapeDtypeStruct((seq_count, row_count, 1), f32),
            jax.ShapeDtypeStruct((row_count, width), bf16),
            jax.ShapeDtypeStruct((row_count, width), bf16),
        ],
        in_specs=[ANY] * 4 + [VMEM] * 4,
        out_specs=[VMEM] * 5,
        scratch_shapes=[
            pltpu.VMEM((pairs, 2, 3, row_count, width), bf16),
            pltpu.VMEM((pairs, 3, row_count, width), bf16),
            pltpu.VMEM((pairs, 3, row_count, width), bf16),
            pltpu.VMEM((3, depth, width), bf16),
            pltpu.VMEM((8, row_count), f32),
            pltpu.VMEM((blk_count, 8, row_count), f32),
            pltpu.VMEM((seq_count, 8, row_count), f32),
        ]
        + semaphores(5 * seq_count + blk_count),
        compiler_params=params(0),
    )(states, *weights, *[g.reshape(1, width) for g in gains], cosine, sine)


def mix_kernel(
    seq_count,
    blk_count,
    weighted_ref,
    stats_ref,
    weight_ref,
    hidden_ref,
    gain_ref,
    mixed_ref,
    partials,
    stats,
    attention,
    weight,
    squares,
    landing,
    parts,
    from_x,
    summed,
    from_z,
    *sems,
):
    seq, grid = Pairs(seq_count), Grid(blk_count)
    row_count, width = attention.shape[1:]
    part_rows, depth = mixed_ref.shape[2:]
    links = Links(*sems)
    load = links.move(weight_ref, weight)

    def stats_for(index):
        return stats_ref.at[:, :, pl.ds(pl.multiple_of(index * row_count, row_count), row_count)]

    own = [
        links.move(weighted_ref.at[seq.me], partials.at[seq.me]),
        links.move(stats_for(seq.me), stats.at[seq.me]),
    ]
    greet([seq.peer(*which) for which in seq.everyone()] + grid.neighbours())
    copies = []
    for which in seq.everyone():
        index = seq.index(*which)
        copies.append(links.send(stats_for(index), stats.at[seq.me], seq.peer(*which)))
        copies.append(links.send(weighted_ref.at[index], partials.at[seq.me], seq.peer(*which)))
    for copy in own:
        copy.wait()
    for copy in copies:
        copy.wait_recv()
    load.wait()
    head_count = width // HD
    shares = []
    for h in range(head_count):
        peaks = [stats[d, h, 0:1, :] for d in range(seq_count)]
        top = functools.reduce(jnp.maximum, peaks)
        scales = [jnp.exp(peak - top) for peak in peaks]
        total = sum(scale * stats[d, h, 1:2, :] for d, scale in enumerate(scales))
        shares += [scale / total for scale in scales]
    shares = columns_of(jnp.concatenate(shares))
    for h in range(head_count):
        merged = jnp.zeros((row_count, HD), jnp.float32)
        for d in range(seq_count):
            column = h * seq_count + d
            merged += (
                partials[d, :, h * HD : (h + 1) * HD].astype(jnp.float32)
                * shares[:, column : column + 1]
            )
        attention[seq.me, :, h * HD : (h + 1) * HD] = merged.astype(jnp.bfloat16)
    block_sum = BlockSum(links, grid, seq, parts, from_x, summed, from_z)

    def use(s):
        block_sum.put(
            s, jnp.dot(attention[s], weight[...], preferred_element_type=jnp.float32)
        )

    share_over_seq(links, seq, attention, use)
    for s, total in block_sum.totals():
        squares[0, s] = jnp.broadcast_to(
            jnp.sum(total * total, axis=1, keepdims=True), (part_rows, HD)
        )
        landing[s] = total
    square_copies = []
    for k, which in enumerate(seq.everyone(), 1):
        square_copies.append(links.send(squares.at[0], squares.at[k], seq.peer(*which)))
    for copy in square_copies:
        copy.wait_recv()
    factor = lax.rsqrt(jnp.sum(squares[...], axis=0) / (depth * seq_count) + EPSILON)
    update = landing[...] * factor[:, :, 0:1] * gain_ref[seq.me]
    mixed_ref[grid.me] = (
        hidden_ref[:, grid.me].astype(jnp.float32) + update
    ).astype(jnp.bfloat16)
    mine = mixed_ref.at[grid.me]
    z_copies = {o: links.send(mine, mine, grid.z_peer(o)) for o in range(1, grid.depth)}
    x_copies = [links.send(mine, mine, grid.x_peer(o)) for o in range(1, grid.width)]
    for o in range(1, grid.depth):
        z_copies[grid.depth - o].wait_recv()
        block = mixed_ref.at[grid.along_z(o) * grid.width + grid.x]
        x_copies += [links.send(block, block, grid.x_peer(x)) for x in range(1, grid.width)]
    for copy in x_copies:
        copy.wait_recv()
    links.finish()


def mix(weighted, stats, weight, hidden, gain, seq_count, blk_count):
    row_count = weighted.shape[1]
    width, depth = weight.shape
    part_rows = row_count // blk_count
    bf16, f32 = jnp.bfloat16, jnp.float32
    return pl.pallas_call(
        functools.partial(mix_kernel, seq_count, blk_count),
        out_shape=jax.ShapeDtypeStruct((blk_count, seq_count, part_rows, depth), bf16),
        in_specs=[ANY] * 3 + [VMEM] * 2,
        out_specs=VMEM,
        scratch_shapes=[
            pltpu.VMEM((seq_count, row_count, width), bf16),
            pltpu.VMEM((seq_count, width // HD, 8, row_count), f32),
            pltpu.VMEM((seq_count, row_count, width), bf16),
            pltpu.VMEM((width, depth), bf16),
            pltpu.VMEM((seq_count, seq_count, part_rows, HD), f32),
            pltpu.VMEM((seq_count, part_rows, depth), f32),
        ]
        + block_sum_scratch(seq_count, blk_count, part_rows, depth)
        + semaphores(4 * seq_count + (seq_count + 3) * blk_count),
        compiler_params=params(1),
    )(
        weighted,
        stats,
        weight,
        hidden.reshape(seq_count, blk_count, part_rows, depth),
        gain.reshape(seq_count, 1, depth),
    )


def feed_kernel(
    seq_count,
    blk_count,
    gate_ref,
    up_ref,
    down_ref,
    mixed_ref,
    gain_ref,
    out_ref,
    gate_up,
    down,
    outgoing,
    from_sibling,
    from_pairs,
    activation,
    halves,
    mixed_parts,
    final_parts,
    parts,
    from_x,
    summed,
    from_z,
    *sems,
):
    seq, grid = Pairs(seq_count), Grid(blk_count)
    part_rows, depth = mixed_ref.shape[2:]
    links = Links(*sems)
    loads = [links.move(gate_ref, gate_up.at[0]), links.move(up_ref, gate_up.at[1])]
    down_load = links.move(down_ref, down)
    greet([seq.peer(*which) for which in seq.everyone()] + grid.neighbours())
    mixed_copies = [
        links.send(
            mixed_ref.at[grid.me, seq.index(*which)], mixed_parts.at[seq.me], seq.peer(*which)
        )
        for which in seq.everyone()
    ]
    mixed_parts[seq.me] = mixed_ref[grid.me, seq.me]
    for load in loads:
        load.wait()

    def partial(offset, other):
        rows = mixed_ref[:, seq.index(offset, other)].astype(jnp.float32)
        rows = rows.reshape(blk_count * part_rows, depth).astype(jnp.bfloat16)
        return [
            lax.dot_general(
                rows, gate_up[k], (((1,), (1,)), ((), ())), preferred_element_type=jnp.float32
            )
            for k in range(2)
        ]

    gate, up = reduce_over_seq(links, seq, partial, outgoing, from_sibling, from_pairs)
    activation[seq.me] = (gate / (1.0 + jnp.exp(-gate)) * up).astype(jnp.bfloat16)
    down_load.wait()
    block_sum = BlockSum(links, grid, seq, parts, from_x, summed, from_z)

    def use(s):
        block_sum.put(
            s, jnp.dot(activation[s], down[...], preferred_element_type=jnp.float32)
        )

    share_over_seq(links, seq, activation, use)
    for s, total in block_sum.totals():
        halves[s] = total.astype(jnp.bfloat16)
    final_parts[seq.me] = halves[seq.me]
    final_copies = [
        links.send(halves.at[seq.index(*which)], final_parts.at[seq.me], seq.peer(*which))
        for which in seq.everyone()
    ]
    for copy in mixed_copies + final_copies:
        copy.wait_recv()
    pieces = [final_parts[d].astype(jnp.float32) for d in range(seq_count)]
    squares = sum(jnp.sum(piece * piece, axis=1, keepdims=True) for piece in pieces)
    factor = lax.rsqrt(squares / (depth * seq_count) + EPSILON)
    for d, piece in enumerate(pieces):
        columns = slice(d * depth, (d + 1) * depth)
        out_ref[:, columns] = (
            mixed_parts[d].astype(jnp.float32) + piece * factor * gain_ref[:, columns]
        ).astype(jnp.bfloat16)
    links.finish()


def feed(gate, up, down, mixed, gain, seq_count, blk_count):
    units, depth = gate.shape
    part_rows = mixed.shape[2]
    row_count = part_rows * blk_count
    pairs = seq_count // 2
    bf16 = jnp.bfloat16
    return pl.pallas_call(
        functools.partial(feed_kernel, seq_count, blk_count),
        out_shape=jax.ShapeDtypeStruct((part_rows, depth * seq_count), bf16),
        in_specs=[ANY] * 3 + [VMEM] * 2,
        out_specs=VMEM,
        scratch_shapes=[
            pltpu.VMEM((2, units, depth), bf16),
            pltpu.VMEM((units, depth), bf16),
            pltpu.VMEM((pairs, 2, 2, row_count, units), bf16),
            pltpu.VMEM((pairs, 2, row_count, units), bf16),
            pltpu.VMEM((pairs, 2, row_count, units), bf16),
            pltpu.VMEM((seq_count, row_count, units), bf16),
            pltpu.VMEM((seq_count, part_rows, depth), bf16),
            pltpu.VMEM((seq_count, part_rows, depth), bf16),
            pltpu.VMEM((seq_count, part_rows, depth), bf16),
        ]
        + block_sum_scratch(seq_count, blk_count, part_rows, depth)
        + semaphores(5 * seq_count + seq_count * blk_count),
        compiler_params=params(2),
    )(gate, up, down, mixed, gain.reshape(1, -1))


def attention_kernel(
    query_ref,
    factor_ref,
    old_limit_ref,
    new_limit_ref,
    picked_ref,
    turn_ref,
    old_keys_ref,
    old_values_ref,
    key_rows_ref,
    value_rows_ref,
    keys_ref,
    values_ref,
    weighted_ref,
    stats_ref,
):
    @pl.when(pl.program_id(1) == 0)
    def blend():
        row_count = key_rows_ref.shape[0]
        token = lax.broadcasted_iota(jnp.int32, (PLEN, row_count), 0)
        hit = token == picked_ref[...]
        chosen = jnp.where(hit, 1.0, 0.0)
        replaced = jnp.max(chosen, axis=1, keepdims=True) > 0.5
        chosen = chosen.astype(jnp.bfloat16)
        old = old_keys_ref[...].astype(jnp.float32)
        turned = old * turn_ref[0:1, :] + pltpu.roll(old, HD // 2, 1) * turn_ref[1:2, :]
        new_keys = jnp.dot(chosen, key_rows_ref[...], preferred_element_type=jnp.float32)
        keys_ref[...] = jnp.where(replaced, new_keys, turned).astype(jnp.bfloat16)
        new_values = jnp.dot(chosen, value_rows_ref[...], preferred_element_type=jnp.float32)
        values_ref[...] = jnp.where(
            replaced, new_values, old_values_ref[...].astype(jnp.float32)
        ).astype(jnp.bfloat16)

    query = (query_ref[...].astype(jnp.float32) * factor_ref[...]).astype(jnp.bfloat16)
    contract = (((1,), (1,)), ((), ()))
    old_scores = lax.dot_general(
        query, keys_ref[...], contract, preferred_element_type=jnp.float32
    )
    new_scores = lax.dot_general(
        query, key_rows_ref[...], contract, preferred_element_type=jnp.float32
    )
    scale = HD ** (-0.5)
    old_seen = lax.broadcasted_iota(jnp.int32, old_scores.shape, 1) <= old_limit_ref[...]
    new_token = lax.broadcasted_iota(jnp.int32, new_scores.shape, 1) - SEL
    new_seen = (new_token >= 0) & (new_token <= new_limit_ref[...])
    old_scores = jnp.where(old_seen, old_scores * scale, MASKED_SCORE)
    new_scores = jnp.where(new_seen, new_scores * scale, MASKED_SCORE)
    peak = jnp.maximum(
        jnp.max(old_scores, axis=1, keepdims=True), jnp.max(new_scores, axis=1, keepdims=True)
    )
    old_weights = jnp.where(old_seen, jnp.exp(old_scores - peak), 0.0)
    new_weights = jnp.where(new_seen, jnp.exp(new_scores - peak), 0.0)
    total = jnp.sum(old_weights, axis=1, keepdims=True) + jnp.sum(
        new_weights, axis=1, keepdims=True
    )
    weighted = jnp.dot(
        old_weights.astype(jnp.bfloat16), values_ref[...], preferred_element_type=jnp.float32
    ) + jnp.dot(
        new_weights.astype(jnp.bfloat16), value_rows_ref[...], preferred_element_type=jnp.float32
    )
    weighted_ref[...] = weighted.astype(jnp.bfloat16)
    lane = lax.broadcasted_iota(jnp.int32, weighted.shape, 1)
    stats = jnp.transpose(jnp.where(lane == 0, peak, total))
    stats_ref[0] = stats[:8, :]


def attend(
    queries, factor, old_limit, new_limit, picked, turn, old_keys, old_values, key_rows, value_rows
):
    total_rows, width = queries.shape
    row_count = key_rows.shape[0]
    head_count = width // HD
    block = min(total_rows, 512)
    by_row = pl.BlockSpec((block, 1), lambda h, i: (i, 0))
    by_head = pl.BlockSpec((PLEN, HD), lambda h, i: (0, h))
    rows_by_head = pl.BlockSpec((row_count, HD), lambda h, i: (0, h))
    tile = pl.BlockSpec((block, HD), lambda h, i: (i, h))
    return pl.pallas_call(
        attention_kernel,
        grid=(head_count, total_rows // block),
        out_shape=[
            jax.ShapeDtypeStruct((PLEN, width), jnp.bfloat16),
            jax.ShapeDtypeStruct((PLEN, width), jnp.bfloat16),
            jax.ShapeDtypeStruct((total_rows, width), jnp.bfloat16),
            jax.ShapeDtypeStruct((head_count, 8, total_rows), jnp.float32),
        ],
        in_specs=[
            tile,
            by_row,
            by_row,
            by_row,
            pl.BlockSpec((1, row_count), lambda h, i: (0, 0)),
            pl.BlockSpec((8, HD), lambda h, i: (0, 0)),
            by_head,
            by_head,
            rows_by_head,
            rows_by_head,
        ],
        out_specs=[
            by_head,
            by_head,
            tile,
            pl.BlockSpec((1, 8, block), lambda h, i: (h, 0, i)),
        ],
        compiler_params=pltpu.CompilerParams(vmem_limit_bytes=48 * 1024 * 1024),
    )(
        queries,
        factor,
        old_limit,
        new_limit,
        picked,
        turn,
        old_keys,
        old_values,
        key_rows,
        value_rows,
    )


def frequencies():
    indices = jnp.arange(HD // 2, dtype=jnp.float32)
    return jnp.exp(indices * (-2.0 * math.log(ROPE_THETA) / HD))


def layout(passage_order, separators, recompute_index, seq_count):
    devices = jnp.arange(seq_count, dtype=jnp.int32)
    slots = jnp.arange(PPR, dtype=jnp.int32)
    earlier = slots[None, :, None] >= slots[None, None, :]
    opening = slots[None, :] * PLEN + jnp.sum(
        jnp.where(earlier, separators[:, None, :], 0), axis=2
    )
    hit = passage_order[None, :] == devices[:, None]
    starts = jnp.sum(jnp.where(hit, opening.reshape(-1)[None, :], 0), axis=1)
    owners = jnp.sum(jnp.where(hit, (devices // PPR)[None, :], 0), axis=1)
    prompt_start = jnp.repeat(opening[:, PPR - 1] + PLEN, PPR)
    offsets = (devices % PPR) * TOKN_DEV
    new_starts = prompt_start + offsets
    new_positions = new_starts[:, None] + jnp.arange(TOKN_DEV, dtype=jnp.int32)[None, :]
    positions = jnp.concatenate([starts[:, None] + recompute_index, new_positions], axis=1)
    requests = jnp.concatenate(
        [
            jnp.broadcast_to(owners[:, None], recompute_index.shape),
            jnp.broadcast_to((devices // PPR)[:, None], new_positions.shape),
        ],
        axis=1,
    )
    return starts, owners, new_starts, offsets, positions, requests


def shards(
    hidden_states,
    query_weight,
    key_weight,
    value_weight,
    output_weight,
    query_gain,
    key_gain,
    attention_gain,
    gate_weight,
    up_weight,
    down_weight,
    feedforward_gain,
    cached_keys,
    cached_values,
    passage_order,
    separators,
    recompute_index,
    prompt_lengths,
):
    seq_count = lax.axis_size("seq")
    blk_count = lax.axis_size("blk")
    seq_index = lax.axis_index("seq")
    row_count = hidden_states.shape[0]
    local_width = query_weight.shape[1]
    total_rows = row_count * seq_count

    def mine(array):
        return lax.dynamic_index_in_dim(array, seq_index, 0, keepdims=False)

    starts, owners, new_starts, offsets, positions, requests = layout(
        passage_order, separators, recompute_index, seq_count
    )
    frequency = frequencies()
    passage_start = mine(starts)
    own_request = seq_index // PPR
    old_limit = jnp.where(requests == mine(owners), positions - passage_start, -1)
    live_limit = lax.dynamic_index_in_dim(prompt_lengths, own_request, 0, False) - 1 - mine(offsets)
    new_limit = jnp.where(
        requests == own_request, jnp.minimum(positions - mine(new_starts), live_limit), -1
    )
    picked = jnp.concatenate(
        [mine(recompute_index), jnp.full((row_count - SEL,), -1, jnp.int32)]
    ).reshape(1, row_count)
    turn_angles = passage_start.astype(jnp.float32) * frequency
    turn_cosine, turn_sine = jnp.cos(turn_angles), jnp.sin(turn_angles)
    turn = jnp.concatenate(
        [
            jnp.concatenate([turn_cosine, turn_cosine])[None],
            jnp.concatenate([-turn_sine, turn_sine])[None],
            jnp.zeros((6, HD), jnp.float32),
        ]
    )
    angles = mine(positions).astype(jnp.float32)[:, None] * frequency[None, :]
    cosine, sine = jnp.cos(angles), jnp.sin(angles)
    hidden, queries, factors, key_rows, value_rows = project(
        hidden_states,
        (query_weight, key_weight, value_weight),
        (query_gain, key_gain),
        jnp.concatenate([cosine, cosine], axis=1),
        jnp.concatenate([-sine, sine], axis=1),
        seq_count,
        blk_count,
    )
    passage_keys, passage_values, weighted, stats = attend(
        queries.reshape(total_rows, local_width),
        factors.reshape(total_rows, 1),
        old_limit.reshape(total_rows, 1),
        new_limit.reshape(total_rows, 1),
        picked,
        turn,
        cached_keys[0],
        cached_values[0],
        key_rows,
        value_rows,
    )
    mixed = mix(
        weighted.reshape(seq_count, row_count, local_width),
        stats,
        output_weight,
        hidden,
        attention_gain,
        seq_count,
        blk_count,
    )
    hidden_out = feed(
        gate_weight.T, up_weight.T, down_weight, mixed, feedforward_gain, seq_count, blk_count
    )
    return (hidden_out, passage_keys[None], passage_values[None])


def solution(mesh):
    return jax.shard_map(
        shards,
        mesh=mesh,
        in_specs=(
            P("seq", None),
            P("seq", "blk"),
            P("seq", "blk"),
            P("seq", "blk"),
            P("blk", "seq"),
            P("blk"),
            P("blk"),
            P(),
            P("seq", "blk"),
            P("seq", "blk"),
            P("blk", "seq"),
            P(),
            P("seq", None, "blk"),
            P("seq", None, "blk"),
            P(),
            P(),
            P(),
            P(),
        ),
        out_specs=(P(("seq", "blk"), None), P("seq", None, "blk"), P("seq", None, "blk")),
        check_vma=False,
    )
```

```python
import functools
import math

import jax
import jax.numpy as jnp
from jax import lax
from jax.experimental import pallas as pl
from jax.experimental.pallas import tpu as pltpu
from jax.sharding import PartitionSpec as P

HD = 128
PLEN = 1024
SEL = 96
PPR = 2
TOKN_DEV = 32

EPSILON = 1e-06
ROPE_THETA = 500000.0
MASKED_SCORE = -1e30
MESH = pl.DeviceIdType.MESH
ANY = pl.BlockSpec(memory_space=pl.ANY)
VMEM = pl.BlockSpec(memory_space=pltpu.VMEM)


def greet(peers):
    barrier = pltpu.get_barrier_semaphore()
    for peer in peers:
        pl.semaphore_signal(barrier, inc=1, device_id=peer, device_id_type=MESH)
    pl.semaphore_wait(barrier, len(peers))


class Links:
    def __init__(self, send_sems, recv_sems, local_sems):
        self.send_sems, self.recv_sems, self.local_sems = send_sems, recv_sems, local_sems
        self.sent, self.moved = 0, 0
        self.unsent, self.started = [], []

    def send(self, source, target, peer):
        copy = pltpu.make_async_remote_copy(
            src_ref=source,
            dst_ref=target,
            send_sem=self.send_sems.at[self.sent],
            recv_sem=self.recv_sems.at[self.sent],
            device_id=peer,
            device_id_type=MESH,
        )
        copy.start()
        self.sent += 1
        self.unsent.append(copy)
        return copy

    def move(self, source, target):
        copy = pltpu.make_async_copy(source, target, self.local_sems.at[self.moved])
        copy.start()
        self.moved += 1
        return copy

    def finish(self):
        for copy in self.unsent:
            copy.wait_send()


class Pairs:
    def __init__(self, count):
        self.count, self.pairs = count, count // 2
        self.me = lax.axis_index("seq")
        self.pair, self.core = lax.div(self.me, 2), lax.rem(self.me, 2)

    def index(self, offset, other):
        core = 1 - self.core if other else self.core
        return lax.rem(self.pair + offset, self.pairs) * 2 + core

    def peer(self, offset, other):
        return {"seq": self.index(offset, other)}

    def everyone(self):
        return [
            (offset, other)
            for offset in list(range(1, self.pairs)) + [0]
            for other in (1, 0)
            if offset or other
        ]

    def source(self, offset, other):
        return ((self.pairs - offset) % self.pairs, other)


class Grid:
    def __init__(self, count):
        self.width = grid_width(count)
        self.depth = count // self.width
        self.me = lax.axis_index("blk")
        self.z, self.x = lax.div(self.me, self.width), lax.rem(self.me, self.width)

    def along_x(self, offset):
        return lax.rem(self.x + offset, self.width)

    def along_z(self, offset):
        return lax.rem(self.z + offset, self.depth)

    def x_peer(self, offset):
        return {"blk": self.z * self.width + self.along_x(offset)}

    def z_peer(self, offset):
        return {"blk": self.along_z(offset) * self.width + self.x}

    def neighbours(self):
        return [self.x_peer(o) for o in range(1, self.width)] + [
            self.z_peer(o) for o in range(1, self.depth)
        ]


def grid_width(count):
    width = 1
    while 8 * width * width <= count:
        width *= 2
    return width


def reduce_over_seq(links, seq, partial, outgoing, from_sibling, from_pairs):
    near, far = {}, []
    order = list(range(1, seq.pairs)) + [0]
    for offset in order:
        for k, piece in enumerate(partial(offset, 1)):
            outgoing[offset, 0, k] = piece.astype(jnp.bfloat16)
        near[offset] = links.send(
            outgoing.at[offset, 0], from_sibling.at[offset], seq.peer(0, 1)
        )
    for offset in order[:-1]:
        pieces = partial(offset, 0)
        near[offset].wait_recv()
        for k, piece in enumerate(pieces):
            outgoing[offset, 1, k] = (piece + from_sibling[offset, k].astype(jnp.float32)).astype(
                jnp.bfloat16
            )
        far.append(
            links.send(outgoing.at[offset, 1], from_pairs.at[offset], seq.peer(offset, 0))
        )
    totals = list(partial(0, 0))
    near[0].wait_recv()
    totals = [t + from_sibling[0, k].astype(jnp.float32) for k, t in enumerate(totals)]
    for offset, copy in zip(order[:-1], far):
        copy.wait_recv()
        totals = [t + from_pairs[offset, k].astype(jnp.float32) for k, t in enumerate(totals)]
    return totals


def share_over_seq(links, seq, buffer, use):
    mine = buffer.at[seq.me]
    far = {o: links.send(mine, mine, seq.peer(o, 0)) for o in range(1, seq.pairs)}
    near = {0: links.send(mine, mine, seq.peer(0, 1))}
    use(seq.me)
    near[0].wait_recv()
    use(seq.index(0, 1))
    for offset in range(1, seq.pairs):
        far[seq.pairs - offset].wait_recv()
        block = buffer.at[seq.index(offset, 0)]
        near[offset] = links.send(block, block, seq.peer(0, 1))
        use(seq.index(offset, 0))
    for offset in range(1, seq.pairs):
        near[offset].wait_recv()
        use(seq.index(offset, 1))


class BlockSum:
    def __init__(self, links, grid, seq, parts, from_x, summed, from_z):
        self.links, self.grid, self.seq = links, grid, seq
        self.parts, self.from_x, self.summed, self.from_z = parts, from_x, summed, from_z
        self.order, self.x_copies, self.z_copies = [], [], []

    def put(self, s, product):
        grid = self.grid
        rows = self.parts.shape[3]
        for z in range(grid.depth):
            for x in range(grid.width):
                at = (z * grid.width + x) * rows
                self.parts[s, z, x] = product[at : at + rows].astype(jnp.bfloat16)
        step = len(self.order)
        self.order.append(s)
        self.x_copies.append(
            [
                self.links.send(
                    self.parts.at[s, :, grid.along_x(o)],
                    self.from_x.at[o, step],
                    grid.x_peer(o),
                )
                for o in range(1, grid.width)
            ]
        )
        if step:
            self.pass_on(step - 1)

    def pass_on(self, step):
        grid = self.grid
        s = self.order[step]
        total = self.parts[s, :, grid.x].astype(jnp.float32)
        for o, copy in enumerate(self.x_copies[step], 1):
            copy.wait_recv()
            total += self.from_x[o, step].astype(jnp.float32)
        self.summed[step] = total.astype(jnp.bfloat16)
        self.z_copies.append(
            [
                self.links.send(
                    self.summed.at[step, grid.along_z(o)],
                    self.from_z.at[o, step],
                    grid.z_peer(o),
                )
                for o in range(1, grid.depth)
            ]
        )

    def totals(self):
        self.pass_on(len(self.order) - 1)
        for step, s in enumerate(self.order):
            total = self.summed[step, self.grid.z].astype(jnp.float32)
            for o, copy in enumerate(self.z_copies[step], 1):
                copy.wait_recv()
                total += self.from_z[o, step].astype(jnp.float32)
            yield s, total


def block_sum_scratch(seq_count, blk_count, part_rows, depth):
    width = grid_width(blk_count)
    height = blk_count // width
    return [
        pltpu.VMEM((seq_count, height, width, part_rows, depth), jnp.bfloat16),
        pltpu.VMEM((width, seq_count, height, part_rows, depth), jnp.bfloat16),
        pltpu.VMEM((seq_count, height, part_rows, depth), jnp.bfloat16),
        pltpu.VMEM((height, seq_count, part_rows, depth), jnp.bfloat16),
    ]


def semaphores(copies):
    return [
        pltpu.SemaphoreType.DMA((copies,)),
        pltpu.SemaphoreType.DMA((copies,)),
        pltpu.SemaphoreType.DMA((8,)),
    ]


def params(collective_id, mebibytes):
    return pltpu.CompilerParams(
        collective_id=collective_id,
        has_side_effects=True,
        vmem_limit_bytes=mebibytes * 1024 * 1024,
    )


def columns_of(rows):
    lanes = rows.shape[1]
    return jnp.transpose(
        jnp.concatenate([rows, jnp.zeros((lanes - rows.shape[0], lanes), jnp.float32)])
    )


def project_kernel(
    seq_count,
    blk_count,
    states_ref,
    query_weight,
    key_weight,
    value_weight,
    query_gain,
    key_gain,
    cosine_ref,
    sine_ref,
    hidden_ref,
    queries_ref,
    factors_ref,
    key_rows_ref,
    value_rows_ref,
    outgoing,
    from_sibling,
    from_pairs,
    weights,
    squares,
    landing,
    sums,
    *sems,
):
    seq = Pairs(seq_count)
    row_count, depth = hidden_ref.shape[1:]
    width = key_rows_ref.shape[1]
    links = Links(*sems)
    blk = lax.axis_index("blk")
    blk_peers = [{"blk": lax.rem(blk + o, blk_count)} for o in range(1, blk_count)]
    loads = [
        links.move(ref, weights.at[k])
        for k, ref in enumerate((query_weight, key_weight, value_weight))
    ]
    own = links.move(
        states_ref.at[:, pl.ds(pl.multiple_of(seq.me * depth, depth), depth)],
        hidden_ref.at[seq.me],
    )
    greet([seq.peer(*which) for which in seq.everyone()] + blk_peers)
    arrivals = {}
    for which in seq.everyone():
        column = pl.multiple_of(seq.index(*which) * depth, depth)
        arrivals[which] = links.send(
            states_ref.at[:, pl.ds(column, depth)], hidden_ref.at[seq.me], seq.peer(*which)
        )
    for load in loads:
        load.wait()

    def partial(offset, other):
        if offset or other:
            arrivals[seq.source(offset, other)].wait_recv()
        else:
            own.wait()
        rows = hidden_ref[seq.index(offset, other)]
        return [
            jnp.dot(rows, weights[k], preferred_element_type=jnp.float32) for k in range(3)
        ]

    query, key, value = reduce_over_seq(links, seq, partial, outgoing, from_sibling, from_pairs)
    value_rows_ref[...] = value.astype(jnp.bfloat16)
    lane = lax.broadcasted_iota(jnp.int32, (row_count, HD), 1)
    query_squares = jnp.sum(query * query, axis=1, keepdims=True)
    key_squares = jnp.sum(key * key, axis=1, keepdims=True)
    squares[...] = jnp.transpose(jnp.where(lane == 0, query_squares, key_squares))[:8]
    parts = [
        links.send(squares, landing.at[o], blk_peers[o - 1]) for o in range(1, blk_count)
    ]

    def turned(raw, gain, h):
        piece = raw[:, h * HD : (h + 1) * HD] * gain[:, h * HD : (h + 1) * HD]
        return piece * cosine_ref[...] + pltpu.roll(piece, HD // 2, 1) * sine_ref[...]

    for h in range(width // HD):
        queries_ref[seq.me, :, h * HD : (h + 1) * HD] = turned(query, query_gain, h).astype(
            jnp.bfloat16
        )
    mine = queries_ref.at[seq.me]
    far = {o: links.send(mine, mine, seq.peer(o, 0)) for o in range(1, seq.pairs)}
    near = [links.send(mine, mine, seq.peer(0, 1))]
    total = squares[...]
    for o, copy in enumerate(parts, 1):
        copy.wait_recv()
        total += landing[o]
    sums[seq.me] = total
    sum_copies = [
        links.send(sums.at[seq.me], sums.at[seq.me], seq.peer(*which))
        for which in seq.everyone()
    ]
    key_factor = lax.rsqrt(columns_of(total) / (width * blk_count) + EPSILON)[:, 1:2]
    for h in range(width // HD):
        key_rows_ref[:, h * HD : (h + 1) * HD] = (turned(key, key_gain, h) * key_factor).astype(
            jnp.bfloat16
        )
    for offset in range(1, seq.pairs):
        far[seq.pairs - offset].wait_recv()
        block = queries_ref.at[seq.index(offset, 0)]
        near.append(links.send(block, block, seq.peer(0, 1)))
    for copy in sum_copies + near:
        copy.wait_recv()
    for d in range(seq_count):
        factors_ref[d] = lax.rsqrt(columns_of(sums[d]) / (width * blk_count) + EPSILON)[:, 0:1]
    links.finish()


def project(states, weights, gains, cosine, sine, seq_count, blk_count):
    row_count = states.shape[0]
    depth, width = weights[0].shape
    pairs = seq_count // 2
    bf16, f32 = jnp.bfloat16, jnp.float32
    return pl.pallas_call(
        functools.partial(project_kernel, seq_count, blk_count),
        out_shape=[
            jax.ShapeDtypeStruct((seq_count, row_count, depth), bf16),
            jax.ShapeDtypeStruct((seq_count, row_count, width), bf16),
            jax.ShapeDtypeStruct((seq_count, row_count, 1), f32),
            jax.ShapeDtypeStruct((row_count, width), bf16),
            jax.ShapeDtypeStruct((row_count, width), bf16),
        ],
        in_specs=[ANY] * 4 + [VMEM] * 4,
        out_specs=[VMEM] * 5,
        scratch_shapes=[
            pltpu.VMEM((pairs, 2, 3, row_count, width), bf16),
            pltpu.VMEM((pairs, 3, row_count, width), bf16),
            pltpu.VMEM((pairs, 3, row_count, width), bf16),
            pltpu.VMEM((3, depth, width), bf16),
            pltpu.VMEM((8, row_count), f32),
            pltpu.VMEM((blk_count, 8, row_count), f32),
            pltpu.VMEM((seq_count, 8, row_count), f32),
        ]
        + semaphores(5 * seq_count + blk_count),
        compiler_params=params(0, 60),
    )(states, *weights, *[g.reshape(1, width) for g in gains], cosine, sine)


def finish_kernel(
    seq_count,
    blk_count,
    weighted_ref,
    stats_ref,
    weight_ref,
    gate_ref,
    up_ref,
    down_ref,
    hidden_ref,
    attention_gain,
    feed_gain,
    out_ref,
    partials,
    stats,
    attention,
    weight,
    squares,
    landing,
    parts,
    from_x,
    summed,
    from_z,
    gate_up,
    down,
    mixed,
    mixed_parts,
    final_parts,
    halves,
    outgoing,
    from_sibling,
    from_pairs,
    activation,
    feed_parts,
    feed_from_x,
    feed_summed,
    feed_from_z,
    *sems,
):
    seq, grid = Pairs(seq_count), Grid(blk_count)
    row_count, width = attention.shape[1:]
    part_rows, depth = mixed.shape[3:]
    links = Links(*sems)
    load = links.move(weight_ref, weight)
    gate_loads = [links.move(gate_ref, gate_up.at[0]), links.move(up_ref, gate_up.at[1])]
    down_load = links.move(down_ref, down)

    def stats_for(index):
        return stats_ref.at[:, :, pl.ds(pl.multiple_of(index * row_count, row_count), row_count)]

    own = [
        links.move(weighted_ref.at[seq.me], partials.at[seq.me]),
        links.move(stats_for(seq.me), stats.at[seq.me]),
    ]
    greet([seq.peer(*which) for which in seq.everyone()] + grid.neighbours())
    copies = []
    for which in seq.everyone():
        index = seq.index(*which)
        copies.append(links.send(stats_for(index), stats.at[seq.me], seq.peer(*which)))
        copies.append(links.send(weighted_ref.at[index], partials.at[seq.me], seq.peer(*which)))
    for copy in own:
        copy.wait()
    for copy in copies:
        copy.wait_recv()
    load.wait()
    head_count = width // HD
    shares = []
    for h in range(head_count):
        peaks = [stats[d, h, 0:1, :] for d in range(seq_count)]
        top = functools.reduce(jnp.maximum, peaks)
        scales = [jnp.exp(peak - top) for peak in peaks]
        total = sum(scale * stats[d, h, 1:2, :] for d, scale in enumerate(scales))
        shares += [scale / total for scale in scales]
    shares = columns_of(jnp.concatenate(shares))
    for h in range(head_count):
        merged = jnp.zeros((row_count, HD), jnp.float32)
        for d in range(seq_count):
            column = h * seq_count + d
            merged += (
                partials[d, :, h * HD : (h + 1) * HD].astype(jnp.float32)
                * shares[:, column : column + 1]
            )
        attention[seq.me, :, h * HD : (h + 1) * HD] = merged.astype(jnp.bfloat16)
    block_sum = BlockSum(links, grid, seq, parts, from_x, summed, from_z)

    def use(s):
        block_sum.put(
            s, jnp.dot(attention[s], weight[...], preferred_element_type=jnp.float32)
        )

    share_over_seq(links, seq, attention, use)
    for s, total in block_sum.totals():
        squares[0, s] = jnp.broadcast_to(
            jnp.sum(total * total, axis=1, keepdims=True), (part_rows, HD)
        )
        landing[s] = total
    square_copies = []
    for k, which in enumerate(seq.everyone(), 1):
        square_copies.append(links.send(squares.at[0], squares.at[k], seq.peer(*which)))
    for copy in square_copies:
        copy.wait_recv()
    factor = lax.rsqrt(jnp.sum(squares[...], axis=0) / (depth * seq_count) + EPSILON)
    update = landing[...] * factor[:, :, 0:1] * attention_gain[seq.me]
    mixed[grid.z, grid.x] = (hidden_ref[:, grid.me].astype(jnp.float32) + update).astype(
        jnp.bfloat16
    )

    chunks = grid.depth
    order = list(range(1, seq.pairs)) + [0]
    mine = mixed.at[grid.z, grid.x]
    x_copies = {0: [links.send(mine, mine, grid.x_peer(o)) for o in range(1, grid.width)]}
    z_copies = {c: links.send(mine, mine, grid.z_peer(chunks - c)) for c in range(1, chunks)}
    mixed_copies = [
        links.send(mixed.at[grid.z, grid.x, seq.index(*which)], mixed_parts.at[seq.me], peer)
        for which, peer in [(which, seq.peer(*which)) for which in seq.everyone()]
    ]
    mixed_parts[seq.me] = mixed[grid.z, grid.x, seq.me]
    for gate_load in gate_loads:
        gate_load.wait()
    down_load.wait()
    near, far, act_far, act_near, part_copies, sum_copies = {}, {}, {}, {}, {}, {}

    def pass_mixed(c):
        z_copies[c].wait_recv()
        block = mixed.at[grid.along_z(c), grid.x]
        x_copies[c] = [links.send(block, block, grid.x_peer(o)) for o in range(1, grid.width)]

    def multiply_gate_up(c):
        for copy in x_copies[c]:
            copy.wait_recv()
        rows = mixed[grid.along_z(c)].astype(jnp.float32)
        rows = rows.reshape(grid.width * seq_count * part_rows, depth).astype(jnp.bfloat16)
        for k in range(2):
            product = lax.dot_general(
                rows, gate_up[k], (((1,), (1,)), ((), ())), preferred_element_type=jnp.float32
            ).astype(jnp.bfloat16)
            for x in range(grid.width):
                for s in range(seq_count):
                    at = (x * seq_count + s) * part_rows
                    outgoing[c, s, k, x] = product[at : at + part_rows]
        for offset in order:
            near[c, offset] = links.send(
                outgoing.at[c, seq.index(offset, 1)],
                from_sibling.at[c, offset],
                seq.peer(0, 1),
            )

    def sum_of_pair(c, offset):
        near[c, offset].wait_recv()
        return outgoing[c, seq.index(offset, 0)].astype(jnp.float32) + from_sibling[
            c, offset
        ].astype(jnp.float32)

    def send_pair_sums(c):
        for offset in order[:-1]:
            outgoing[c, seq.index(offset, 0)] = sum_of_pair(c, offset).astype(jnp.bfloat16)
            far[c, offset] = links.send(
                outgoing.at[c, seq.index(offset, 0)],
                from_pairs.at[c, offset],
                seq.peer(offset, 0),
            )

    def activate(c):
        total = sum_of_pair(c, 0)
        for offset in order[:-1]:
            far[c, offset].wait_recv()
            total += from_pairs[c, offset].astype(jnp.float32)
        gate, up = total[0], total[1]
        activation[c, seq.me] = (gate / (1.0 + jnp.exp(-gate)) * up).astype(jnp.bfloat16)
        block = activation.at[c, seq.me]
        for offset in order[:-1]:
            act_far[c, offset] = links.send(block, block, seq.peer(offset, 0))
        act_near[c] = [links.send(block, block, seq.peer(0, 1))]

    def multiply_down(c):
        for offset in order[:-1]:
            act_far[c, seq.pairs - offset].wait_recv()
            block = activation.at[c, seq.index(offset, 0)]
            act_near[c].append(links.send(block, block, seq.peer(0, 1)))
        for copy in act_near[c]:
            copy.wait_recv()
        rows = activation[c].astype(jnp.float32)
        rows = rows.reshape(seq_count * grid.width * part_rows, rows.shape[-1])
        product = jnp.dot(
            rows.astype(jnp.bfloat16), down[...], preferred_element_type=jnp.float32
        ).astype(jnp.bfloat16)
        for s in range(seq_count):
            for x in range(grid.width):
                at = (s * grid.width + x) * part_rows
                feed_parts[c, x, s] = product[at : at + part_rows]
        part_copies[c] = [
            links.send(
                feed_parts.at[c, grid.along_x(o)], feed_from_x.at[c, o], grid.x_peer(o)
            )
            for o in range(1, grid.width)
        ]

    def sum_over_x(c):
        total = feed_parts[c, grid.x].astype(jnp.float32)
        for o, copy in enumerate(part_copies[c], 1):
            copy.wait_recv()
            total += feed_from_x[c, o].astype(jnp.float32)
        feed_summed[c] = total.astype(jnp.bfloat16)
        if c:
            sum_copies[c] = links.send(feed_summed.at[c], feed_from_z.at[c], grid.z_peer(c))

    for step in range(chunks + 3):
        if step < chunks:
            multiply_gate_up(step)
            if step + 1 < chunks:
                pass_mixed(step + 1)
            send_pair_sums(step)
        if 0 <= step - 1 < chunks:
            activate(step - 1)
        if 0 <= step - 2 < chunks:
            multiply_down(step - 2)
        if 0 <= step - 3 < chunks:
            sum_over_x(step - 3)
    total = feed_summed[0].astype(jnp.float32)
    for c in range(1, chunks):
        sum_copies[c].wait_recv()
        total += feed_from_z[c].astype(jnp.float32)
    halves[...] = total.astype(jnp.bfloat16)
    final_parts[seq.me] = halves[seq.me]
    final_copies = [
        links.send(halves.at[seq.index(*which)], final_parts.at[seq.me], seq.peer(*which))
        for which in seq.everyone()
    ]
    for copy in mixed_copies + final_copies:
        copy.wait_recv()
    pieces = [final_parts[d].astype(jnp.float32) for d in range(seq_count)]
    squares_total = sum(jnp.sum(piece * piece, axis=1, keepdims=True) for piece in pieces)
    factor = lax.rsqrt(squares_total / (depth * seq_count) + EPSILON)
    for d, piece in enumerate(pieces):
        columns = slice(d * depth, (d + 1) * depth)
        out_ref[:, columns] = (
            mixed_parts[d].astype(jnp.float32) + piece * factor * feed_gain[:, columns]
        ).astype(jnp.bfloat16)
    links.finish()


def finish(weighted, stats, weights, hidden, gains, seq_count, blk_count):
    row_count = weighted.shape[1]
    width, depth = weights[0].shape
    units = weights[1].shape[0]
    part_rows = row_count // blk_count
    pairs = seq_count // 2
    across = grid_width(blk_count)
    chunks = blk_count // across
    bf16, f32 = jnp.bfloat16, jnp.float32
    return pl.pallas_call(
        functools.partial(finish_kernel, seq_count, blk_count),
        out_shape=jax.ShapeDtypeStruct((part_rows, depth * seq_count), bf16),
        in_specs=[ANY] * 6 + [VMEM] * 3,
        out_specs=VMEM,
        scratch_shapes=[
            pltpu.VMEM((seq_count, row_count, width), bf16),
            pltpu.VMEM((seq_count, width // HD, 8, row_count), f32),
            pltpu.VMEM((seq_count, row_count, width), bf16),
            pltpu.VMEM((width, depth), bf16),
            pltpu.VMEM((seq_count, seq_count, part_rows, HD), f32),
            pltpu.VMEM((seq_count, part_rows, depth), f32),
        ]
        + block_sum_scratch(seq_count, blk_count, part_rows, depth)
        + [
            pltpu.VMEM((2, units, depth), bf16),
            pltpu.VMEM((units, depth), bf16),
            pltpu.VMEM((chunks, across, seq_count, part_rows, depth), bf16),
            pltpu.VMEM((seq_count, part_rows, depth), bf16),
            pltpu.VMEM((seq_count, part_rows, depth), bf16),
            pltpu.VMEM((seq_count, part_rows, depth), bf16),
            pltpu.VMEM((chunks, seq_count, 2, across, part_rows, units), bf16),
            pltpu.VMEM((chunks, pairs, 2, across, part_rows, units), bf16),
            pltpu.VMEM((chunks, pairs, 2, across, part_rows, units), bf16),
            pltpu.VMEM((chunks, seq_count, across, part_rows, units), bf16),
            pltpu.VMEM((chunks, across, seq_count, part_rows, depth), bf16),
            pltpu.VMEM((chunks, across, seq_count, part_rows, depth), bf16),
            pltpu.VMEM((chunks, seq_count, part_rows, depth), bf16),
            pltpu.VMEM((chunks, seq_count, part_rows, depth), bf16),
        ]
        + semaphores(8 * seq_count + (2 * seq_count + 3) * blk_count),
        compiler_params=params(1, 48),
    )(
        weighted,
        stats,
        *weights,
        hidden.reshape(seq_count, blk_count, part_rows, depth),
        gains[0].reshape(seq_count, 1, depth),
        gains[1].reshape(1, -1),
    )


def attention_kernel(
    query_ref,
    factor_ref,
    old_limit_ref,
    new_limit_ref,
    picked_ref,
    turn_ref,
    old_keys_ref,
    old_values_ref,
    key_rows_ref,
    value_rows_ref,
    keys_ref,
    values_ref,
    weighted_ref,
    stats_ref,
):
    @pl.when(pl.program_id(1) == 0)
    def blend():
        row_count = key_rows_ref.shape[0]
        token = lax.broadcasted_iota(jnp.int32, (PLEN, row_count), 0)
        hit = token == picked_ref[...]
        chosen = jnp.where(hit, 1.0, 0.0)
        replaced = jnp.max(chosen, axis=1, keepdims=True) > 0.5
        chosen = chosen.astype(jnp.bfloat16)
        old = old_keys_ref[...].astype(jnp.float32)
        turned = old * turn_ref[0:1, :] + pltpu.roll(old, HD // 2, 1) * turn_ref[1:2, :]
        new_keys = jnp.dot(chosen, key_rows_ref[...], preferred_element_type=jnp.float32)
        keys_ref[...] = jnp.where(replaced, new_keys, turned).astype(jnp.bfloat16)
        new_values = jnp.dot(chosen, value_rows_ref[...], preferred_element_type=jnp.float32)
        values_ref[...] = jnp.where(
            replaced, new_values, old_values_ref[...].astype(jnp.float32)
        ).astype(jnp.bfloat16)

    query = (query_ref[...].astype(jnp.float32) * factor_ref[...]).astype(jnp.bfloat16)
    contract = (((1,), (1,)), ((), ()))
    old_scores = lax.dot_general(
        query, keys_ref[...], contract, preferred_element_type=jnp.float32
    )
    new_scores = lax.dot_general(
        query, key_rows_ref[...], contract, preferred_element_type=jnp.float32
    )
    scale = HD ** (-0.5)
    old_seen = lax.broadcasted_iota(jnp.int32, old_scores.shape, 1) <= old_limit_ref[...]
    new_token = lax.broadcasted_iota(jnp.int32, new_scores.shape, 1) - SEL
    new_seen = (new_token >= 0) & (new_token <= new_limit_ref[...])
    old_scores = jnp.where(old_seen, old_scores * scale, MASKED_SCORE)
    new_scores = jnp.where(new_seen, new_scores * scale, MASKED_SCORE)
    peak = jnp.maximum(
        jnp.max(old_scores, axis=1, keepdims=True), jnp.max(new_scores, axis=1, keepdims=True)
    )
    old_weights = jnp.where(old_seen, jnp.exp(old_scores - peak), 0.0)
    new_weights = jnp.where(new_seen, jnp.exp(new_scores - peak), 0.0)
    total = jnp.sum(old_weights, axis=1, keepdims=True) + jnp.sum(
        new_weights, axis=1, keepdims=True
    )
    weighted = jnp.dot(
        old_weights.astype(jnp.bfloat16), values_ref[...], preferred_element_type=jnp.float32
    ) + jnp.dot(
        new_weights.astype(jnp.bfloat16), value_rows_ref[...], preferred_element_type=jnp.float32
    )
    weighted_ref[...] = weighted.astype(jnp.bfloat16)
    lane = lax.broadcasted_iota(jnp.int32, weighted.shape, 1)
    stats = jnp.transpose(jnp.where(lane == 0, peak, total))
    stats_ref[0] = stats[:8, :]


def attend(
    queries, factor, old_limit, new_limit, picked, turn, old_keys, old_values, key_rows, value_rows
):
    total_rows, width = queries.shape
    row_count = key_rows.shape[0]
    head_count = width // HD
    block = min(total_rows, 512)
    by_row = pl.BlockSpec((block, 1), lambda h, i: (i, 0))
    by_head = pl.BlockSpec((PLEN, HD), lambda h, i: (0, h))
    rows_by_head = pl.BlockSpec((row_count, HD), lambda h, i: (0, h))
    tile = pl.BlockSpec((block, HD), lambda h, i: (i, h))
    return pl.pallas_call(
        attention_kernel,
        grid=(head_count, total_rows // block),
        out_shape=[
            jax.ShapeDtypeStruct((PLEN, width), jnp.bfloat16),
            jax.ShapeDtypeStruct((PLEN, width), jnp.bfloat16),
            jax.ShapeDtypeStruct((total_rows, width), jnp.bfloat16),
            jax.ShapeDtypeStruct((head_count, 8, total_rows), jnp.float32),
        ],
        in_specs=[
            tile,
            by_row,
            by_row,
            by_row,
            pl.BlockSpec((1, row_count), lambda h, i: (0, 0)),
            pl.BlockSpec((8, HD), lambda h, i: (0, 0)),
            by_head,
            by_head,
            rows_by_head,
            rows_by_head,
        ],
        out_specs=[
            by_head,
            by_head,
            tile,
            pl.BlockSpec((1, 8, block), lambda h, i: (h, 0, i)),
        ],
        compiler_params=pltpu.CompilerParams(vmem_limit_bytes=48 * 1024 * 1024),
    )(
        queries,
        factor,
        old_limit,
        new_limit,
        picked,
        turn,
        old_keys,
        old_values,
        key_rows,
        value_rows,
    )


def frequencies():
    indices = jnp.arange(HD // 2, dtype=jnp.float32)
    return jnp.exp(indices * (-2.0 * math.log(ROPE_THETA) / HD))


def layout(passage_order, separators, recompute_index, seq_count):
    devices = jnp.arange(seq_count, dtype=jnp.int32)
    slots = jnp.arange(PPR, dtype=jnp.int32)
    earlier = slots[None, :, None] >= slots[None, None, :]
    opening = slots[None, :] * PLEN + jnp.sum(
        jnp.where(earlier, separators[:, None, :], 0), axis=2
    )
    hit = passage_order[None, :] == devices[:, None]
    starts = jnp.sum(jnp.where(hit, opening.reshape(-1)[None, :], 0), axis=1)
    owners = jnp.sum(jnp.where(hit, (devices // PPR)[None, :], 0), axis=1)
    prompt_start = jnp.repeat(opening[:, PPR - 1] + PLEN, PPR)
    offsets = (devices % PPR) * TOKN_DEV
    new_starts = prompt_start + offsets
    new_positions = new_starts[:, None] + jnp.arange(TOKN_DEV, dtype=jnp.int32)[None, :]
    positions = jnp.concatenate([starts[:, None] + recompute_index, new_positions], axis=1)
    requests = jnp.concatenate(
        [
            jnp.broadcast_to(owners[:, None], recompute_index.shape),
            jnp.broadcast_to((devices // PPR)[:, None], new_positions.shape),
        ],
        axis=1,
    )
    return starts, owners, new_starts, offsets, positions, requests


def shards(
    hidden_states,
    query_weight,
    key_weight,
    value_weight,
    output_weight,
    query_gain,
    key_gain,
    attention_gain,
    gate_weight,
    up_weight,
    down_weight,
    feedforward_gain,
    cached_keys,
    cached_values,
    passage_order,
    separators,
    recompute_index,
    prompt_lengths,
):
    seq_count = lax.axis_size("seq")
    blk_count = lax.axis_size("blk")
    seq_index = lax.axis_index("seq")
    row_count = hidden_states.shape[0]
    local_width = query_weight.shape[1]
    total_rows = row_count * seq_count

    def mine(array):
        return lax.dynamic_index_in_dim(array, seq_index, 0, keepdims=False)

    starts, owners, new_starts, offsets, positions, requests = layout(
        passage_order, separators, recompute_index, seq_count
    )
    frequency = frequencies()
    passage_start = mine(starts)
    own_request = seq_index // PPR
    old_limit = jnp.where(requests == mine(owners), positions - passage_start, -1)
    live_limit = lax.dynamic_index_in_dim(prompt_lengths, own_request, 0, False) - 1 - mine(offsets)
    new_limit = jnp.where(
        requests == own_request, jnp.minimum(positions - mine(new_starts), live_limit), -1
    )
    picked = jnp.concatenate(
        [mine(recompute_index), jnp.full((row_count - SEL,), -1, jnp.int32)]
    ).reshape(1, row_count)
    turn_angles = passage_start.astype(jnp.float32) * frequency
    turn_cosine, turn_sine = jnp.cos(turn_angles), jnp.sin(turn_angles)
    turn = jnp.concatenate(
        [
            jnp.concatenate([turn_cosine, turn_cosine])[None],
            jnp.concatenate([-turn_sine, turn_sine])[None],
            jnp.zeros((6, HD), jnp.float32),
        ]
    )
    angles = mine(positions).astype(jnp.float32)[:, None] * frequency[None, :]
    cosine, sine = jnp.cos(angles), jnp.sin(angles)
    hidden, queries, factors, key_rows, value_rows = project(
        hidden_states,
        (query_weight, key_weight, value_weight),
        (query_gain, key_gain),
        jnp.concatenate([cosine, cosine], axis=1),
        jnp.concatenate([-sine, sine], axis=1),
        seq_count,
        blk_count,
    )
    passage_keys, passage_values, weighted, stats = attend(
        queries.reshape(total_rows, local_width),
        factors.reshape(total_rows, 1),
        old_limit.reshape(total_rows, 1),
        new_limit.reshape(total_rows, 1),
        picked,
        turn,
        cached_keys[0],
        cached_values[0],
        key_rows,
        value_rows,
    )
    hidden_out = finish(
        weighted.reshape(seq_count, row_count, local_width),
        stats,
        (output_weight, gate_weight.T, up_weight.T, down_weight),
        hidden,
        (attention_gain, feedforward_gain),
        seq_count,
        blk_count,
    )
    return (hidden_out, passage_keys[None], passage_values[None])


def solution(mesh):
    return jax.shard_map(
        shards,
        mesh=mesh,
        in_specs=(
            P("seq", None),
            P("seq", "blk"),
            P("seq", "blk"),
            P("seq", "blk"),
            P("blk", "seq"),
            P("blk"),
            P("blk"),
            P(),
            P("seq", "blk"),
            P("seq", "blk"),
            P("blk", "seq"),
            P(),
            P("seq", None, "blk"),
            P("seq", None, "blk"),
            P(),
            P(),
            P(),
            P(),
        ),
        out_specs=(P(("seq", "blk"), None), P("seq", None, "blk"), P("seq", None, "blk")),
        check_vma=False,
    )
```

```python
import functools

import jax
import jax.numpy as jnp
import numpy as np
from jax import lax
from jax.experimental import pallas as pl
from jax.experimental.pallas import tpu as pltpu
from jax.sharding import PartitionSpec as P

HD = 128
PLEN = 1024
SEL = 96
PPR = 2
TOKN_DEV = 32

EPSILON = 1e-06
ROPE_THETA = 500000.0
MASKED_SCORE = -1e30
MESH = pl.DeviceIdType.MESH
ANY = pl.BlockSpec(memory_space=pl.ANY)
VMEM = pl.BlockSpec(memory_space=pltpu.VMEM)
SMEM = pl.BlockSpec(memory_space=pltpu.SMEM)


def greet(peers):
    barrier = pltpu.get_barrier_semaphore()
    for peer in peers:
        pl.semaphore_signal(barrier, inc=1, device_id=peer, device_id_type=MESH)
    pl.semaphore_wait(barrier, len(peers))


class Links:
    def __init__(self, send_sems, recv_sems, local_sems):
        self.send_sems, self.recv_sems, self.local_sems = send_sems, recv_sems, local_sems
        self.sent, self.moved = 0, 0
        self.unsent, self.started = [], []

    def send(self, source, target, peer):
        copy = pltpu.make_async_remote_copy(
            src_ref=source,
            dst_ref=target,
            send_sem=self.send_sems.at[self.sent],
            recv_sem=self.recv_sems.at[self.sent],
            device_id=peer,
            device_id_type=MESH,
        )
        copy.start()
        self.sent += 1
        self.unsent.append(copy)
        return copy

    def move(self, source, target):
        copy = pltpu.make_async_copy(source, target, self.local_sems.at[self.moved])
        copy.start()
        self.moved += 1
        return copy

    def finish(self):
        for copy in self.unsent:
            copy.wait_send()


class Pairs:
    def __init__(self, count):
        self.count, self.pairs = count, count // 2
        self.me = lax.axis_index("seq")
        self.pair, self.core = lax.div(self.me, 2), lax.rem(self.me, 2)

    def index(self, offset, other):
        core = 1 - self.core if other else self.core
        return lax.rem(self.pair + offset, self.pairs) * 2 + core

    def peer(self, offset, other):
        return {"seq": self.index(offset, other)}

    def everyone(self):
        return [
            (offset, other)
            for offset in list(range(1, self.pairs)) + [0]
            for other in (1, 0)
            if offset or other
        ]

    def source(self, offset, other):
        return ((self.pairs - offset) % self.pairs, other)


class Grid:
    def __init__(self, count):
        self.width = grid_width(count)
        self.depth = count // self.width
        self.me = lax.axis_index("blk")
        self.z, self.x = lax.div(self.me, self.width), lax.rem(self.me, self.width)

    def along_x(self, offset):
        return lax.rem(self.x + offset, self.width)

    def along_z(self, offset):
        return lax.rem(self.z + offset, self.depth)

    def x_peer(self, offset):
        return {"blk": self.z * self.width + self.along_x(offset)}

    def z_peer(self, offset):
        return {"blk": self.along_z(offset) * self.width + self.x}

    def neighbours(self):
        return [self.x_peer(o) for o in range(1, self.width)] + [
            self.z_peer(o) for o in range(1, self.depth)
        ]


def grid_width(count):
    width = 1
    while 8 * width * width <= count:
        width *= 2
    return width


def reduce_over_seq(links, seq, partial, outgoing, from_sibling, from_pairs):
    near, far = {}, []
    order = list(range(1, seq.pairs)) + [0]
    for offset in order:
        for k, piece in enumerate(partial(offset, 1)):
            outgoing[offset, 0, k] = piece.astype(jnp.bfloat16)
        near[offset] = links.send(
            outgoing.at[offset, 0], from_sibling.at[offset], seq.peer(0, 1)
        )
    for offset in order[:-1]:
        pieces = partial(offset, 0)
        near[offset].wait_recv()
        for k, piece in enumerate(pieces):
            outgoing[offset, 1, k] = (piece + from_sibling[offset, k].astype(jnp.float32)).astype(
                jnp.bfloat16
            )
        far.append(
            links.send(outgoing.at[offset, 1], from_pairs.at[offset], seq.peer(offset, 0))
        )
    totals = list(partial(0, 0))
    near[0].wait_recv()
    totals = [t + from_sibling[0, k].astype(jnp.float32) for k, t in enumerate(totals)]
    for offset, copy in zip(order[:-1], far):
        copy.wait_recv()
        totals = [t + from_pairs[offset, k].astype(jnp.float32) for k, t in enumerate(totals)]
    return totals


def share_over_seq(links, seq, buffer, use):
    mine = buffer.at[seq.me]
    far = {o: links.send(mine, mine, seq.peer(o, 0)) for o in range(1, seq.pairs)}
    near = {0: links.send(mine, mine, seq.peer(0, 1))}
    use(seq.me)
    near[0].wait_recv()
    use(seq.index(0, 1))
    for offset in range(1, seq.pairs):
        far[seq.pairs - offset].wait_recv()
        block = buffer.at[seq.index(offset, 0)]
        near[offset] = links.send(block, block, seq.peer(0, 1))
        use(seq.index(offset, 0))
    for offset in range(1, seq.pairs):
        near[offset].wait_recv()
        use(seq.index(offset, 1))


class BlockSum:
    def __init__(self, links, grid, seq, parts, from_x, summed, from_z):
        self.links, self.grid, self.seq = links, grid, seq
        self.parts, self.from_x, self.summed, self.from_z = parts, from_x, summed, from_z
        self.order, self.x_copies, self.z_copies = [], [], []

    def put(self, s, product):
        grid = self.grid
        rows = self.parts.shape[3]
        for z in range(grid.depth):
            for x in range(grid.width):
                at = (z * grid.width + x) * rows
                self.parts[s, z, x] = product[at : at + rows].astype(jnp.bfloat16)
        step = len(self.order)
        self.order.append(s)
        self.x_copies.append(
            [
                self.links.send(
                    self.parts.at[s, :, grid.along_x(o)],
                    self.from_x.at[o, step],
                    grid.x_peer(o),
                )
                for o in range(1, grid.width)
            ]
        )
        if step:
            self.pass_on(step - 1)

    def pass_on(self, step):
        grid = self.grid
        s = self.order[step]
        total = self.parts[s, :, grid.x].astype(jnp.float32)
        for o, copy in enumerate(self.x_copies[step], 1):
            copy.wait_recv()
            total += self.from_x[o, step].astype(jnp.float32)
        self.summed[step] = total.astype(jnp.bfloat16)
        self.z_copies.append(
            [
                self.links.send(
                    self.summed.at[step, grid.along_z(o)],
                    self.from_z.at[o, step],
                    grid.z_peer(o),
                )
                for o in range(1, grid.depth)
            ]
        )

    def totals(self):
        self.pass_on(len(self.order) - 1)
        for step, s in enumerate(self.order):
            total = self.summed[step, self.grid.z].astype(jnp.float32)
            for o, copy in enumerate(self.z_copies[step], 1):
                copy.wait_recv()
                total += self.from_z[o, step].astype(jnp.float32)
            yield s, total


def block_sum_scratch(seq_count, blk_count, part_rows, depth):
    width = grid_width(blk_count)
    height = blk_count // width
    return [
        pltpu.VMEM((seq_count, height, width, part_rows, depth), jnp.bfloat16),
        pltpu.VMEM((width, seq_count, height, part_rows, depth), jnp.bfloat16),
        pltpu.VMEM((seq_count, height, part_rows, depth), jnp.bfloat16),
        pltpu.VMEM((height, seq_count, part_rows, depth), jnp.bfloat16),
    ]


def semaphores(copies):
    return [
        pltpu.SemaphoreType.DMA((copies,)),
        pltpu.SemaphoreType.DMA((copies,)),
        pltpu.SemaphoreType.DMA((8,)),
    ]


def params(collective_id, mebibytes):
    return pltpu.CompilerParams(
        collective_id=collective_id,
        has_side_effects=True,
        vmem_limit_bytes=mebibytes * 1024 * 1024,
    )


def columns_of(rows):
    lanes = rows.shape[1]
    return jnp.transpose(
        jnp.concatenate([rows, jnp.zeros((lanes - rows.shape[0], lanes), jnp.float32)])
    )


def project_kernel(
    seq_count,
    blk_count,
    states_ref,
    query_weight,
    key_weight,
    value_weight,
    query_gain,
    key_gain,
    frequency_ref,
    recompute_ref,
    order_ref,
    separators_ref,
    lengths_ref,
    hidden_ref,
    queries_ref,
    factors_ref,
    key_rows_ref,
    value_rows_ref,
    old_limit_ref,
    new_limit_ref,
    picked_ref,
    turn_ref,
    outgoing,
    from_sibling,
    from_pairs,
    weights,
    squares,
    landing,
    sums,
    chosen,
    *sems,
):
    seq = Pairs(seq_count)
    row_count, depth = hidden_ref.shape[1:]
    width = key_rows_ref.shape[1]
    links = Links(*sems)
    blk = lax.axis_index("blk")
    blk_peers = [{"blk": lax.rem(blk + o, blk_count)} for o in range(1, blk_count)]
    loads = [
        links.move(ref, weights.at[k])
        for k, ref in enumerate((query_weight, key_weight, value_weight))
    ]
    own = links.move(
        states_ref.at[:, pl.ds(pl.multiple_of(seq.me * depth, depth), depth)],
        hidden_ref.at[seq.me],
    )
    greet([seq.peer(*which) for which in seq.everyone()] + blk_peers)
    arrivals = {}
    for which in seq.everyone():
        column = pl.multiple_of(seq.index(*which) * depth, depth)
        arrivals[which] = links.send(
            states_ref.at[:, pl.ds(column, depth)], hidden_ref.at[seq.me], seq.peer(*which)
        )
    chosen[:, :SEL] = recompute_ref[...]
    lane = lax.broadcasted_iota(jnp.int32, (1, row_count), 1)
    limits, my_positions, my_start, my_picked = layout(
        seq.me, seq_count, order_ref, separators_ref, lengths_ref, chosen, lane
    )
    picked_ref[...] = jnp.where(lane < SEL, my_picked, -1)
    limits = columns_of(jnp.concatenate(limits + [my_positions]).astype(jnp.float32))
    for d in range(seq_count):
        old_limit_ref[d] = limits[:, 2 * d : 2 * d + 1]
        new_limit_ref[d] = limits[:, 2 * d + 1 : 2 * d + 2]
    frequency = frequency_ref[...]
    side = jnp.where(lane < HD // 2, -1.0, 1.0)
    turn_angles = my_start.astype(jnp.float32) * frequency
    turn_ref[0:1, :] = jnp.cos(turn_angles)
    turn_ref[1:2, :] = jnp.sin(turn_angles) * side
    angles = limits[:, 2 * seq_count : 2 * seq_count + 1] * frequency
    cosine, sine = jnp.cos(angles), jnp.sin(angles) * side
    for load in loads:
        load.wait()

    def partial(offset, other):
        if offset or other:
            arrivals[seq.source(offset, other)].wait_recv()
        else:
            own.wait()
        rows = hidden_ref[seq.index(offset, other)]
        return [
            jnp.dot(rows, weights[k], preferred_element_type=jnp.float32) for k in range(3)
        ]

    query, key, value = reduce_over_seq(links, seq, partial, outgoing, from_sibling, from_pairs)
    value_rows_ref[...] = value.astype(jnp.bfloat16)
    lane = lax.broadcasted_iota(jnp.int32, (row_count, HD), 1)
    query_squares = jnp.sum(query * query, axis=1, keepdims=True)
    key_squares = jnp.sum(key * key, axis=1, keepdims=True)
    squares[...] = jnp.transpose(jnp.where(lane == 0, query_squares, key_squares))[:8]
    parts = [
        links.send(squares, landing.at[o], blk_peers[o - 1]) for o in range(1, blk_count)
    ]

    def turned(raw, gain, h):
        piece = raw[:, h * HD : (h + 1) * HD] * gain[:, h * HD : (h + 1) * HD]
        return piece * cosine + pltpu.roll(piece, HD // 2, 1) * sine

    for h in range(width // HD):
        queries_ref[seq.me, :, h * HD : (h + 1) * HD] = turned(query, query_gain, h).astype(
            jnp.bfloat16
        )
    mine = queries_ref.at[seq.me]
    far = {o: links.send(mine, mine, seq.peer(o, 0)) for o in range(1, seq.pairs)}
    near = [links.send(mine, mine, seq.peer(0, 1))]
    total = squares[...]
    for o, copy in enumerate(parts, 1):
        copy.wait_recv()
        total += landing[o]
    sums[seq.me] = total
    sum_copies = [
        links.send(sums.at[seq.me], sums.at[seq.me], seq.peer(*which))
        for which in seq.everyone()
    ]
    key_factor = lax.rsqrt(columns_of(total) / (width * blk_count) + EPSILON)[:, 1:2]
    for h in range(width // HD):
        key_rows_ref[:, h * HD : (h + 1) * HD] = (turned(key, key_gain, h) * key_factor).astype(
            jnp.bfloat16
        )
    for offset in range(1, seq.pairs):
        far[seq.pairs - offset].wait_recv()
        block = queries_ref.at[seq.index(offset, 0)]
        near.append(links.send(block, block, seq.peer(0, 1)))
    for copy in sum_copies + near:
        copy.wait_recv()
    for d in range(seq_count):
        factors_ref[d] = lax.rsqrt(columns_of(sums[d]) / (width * blk_count) + EPSILON)[:, 0:1]
    links.finish()


def project(
    states, weights, gains, recompute_index, passage_order, separators, lengths, seq_count, blk_count
):
    row_count = states.shape[0]
    depth, width = weights[0].shape
    pairs = seq_count // 2
    bf16, f32 = jnp.bfloat16, jnp.float32
    return pl.pallas_call(
        functools.partial(project_kernel, seq_count, blk_count),
        out_shape=[
            jax.ShapeDtypeStruct((seq_count, row_count, depth), bf16),
            jax.ShapeDtypeStruct((seq_count, row_count, width), bf16),
            jax.ShapeDtypeStruct((seq_count, row_count, 1), f32),
            jax.ShapeDtypeStruct((row_count, width), bf16),
            jax.ShapeDtypeStruct((row_count, width), bf16),
            jax.ShapeDtypeStruct((seq_count, row_count, 1), f32),
            jax.ShapeDtypeStruct((seq_count, row_count, 1), f32),
            jax.ShapeDtypeStruct((1, row_count), jnp.int32),
            jax.ShapeDtypeStruct((8, HD), f32),
        ],
        in_specs=[ANY] * 4 + [VMEM] * 4 + [SMEM] * 3,
        out_specs=[VMEM] * 9,
        scratch_shapes=[
            pltpu.VMEM((pairs, 2, 3, row_count, width), bf16),
            pltpu.VMEM((pairs, 3, row_count, width), bf16),
            pltpu.VMEM((pairs, 3, row_count, width), bf16),
            pltpu.VMEM((3, depth, width), bf16),
            pltpu.VMEM((8, row_count), f32),
            pltpu.VMEM((blk_count, 8, row_count), f32),
            pltpu.VMEM((seq_count, 8, row_count), f32),
            pltpu.VMEM((seq_count, row_count), jnp.int32),
        ]
        + semaphores(5 * seq_count + blk_count),
        compiler_params=params(0, 60),
    )(
        states,
        *weights,
        *[g.reshape(1, width) for g in gains],
        frequencies(),
        recompute_index,
        passage_order,
        separators,
        lengths,
    )


def finish_kernel(
    seq_count,
    blk_count,
    weighted_ref,
    stats_ref,
    weight_ref,
    gate_ref,
    up_ref,
    down_ref,
    hidden_ref,
    attention_gain,
    feed_gain,
    out_ref,
    partials,
    stats,
    attention,
    weight,
    squares,
    landing,
    hidden,
    parts,
    from_x,
    summed,
    from_z,
    gate_up,
    down,
    mixed,
    mixed_parts,
    final_parts,
    halves,
    outgoing,
    from_sibling,
    from_pairs,
    activation,
    feed_parts,
    feed_from_x,
    feed_summed,
    feed_from_z,
    *sems,
):
    seq, grid = Pairs(seq_count), Grid(blk_count)
    row_count, width = attention.shape[1:]
    part_rows, depth = mixed.shape[3:]
    links = Links(*sems)
    load = links.move(weight_ref, weight)
    gate_loads = [links.move(gate_ref, gate_up.at[0]), links.move(up_ref, gate_up.at[1])]
    down_load = links.move(down_ref, down)
    hidden_load = links.move(hidden_ref.at[:, grid.me], hidden)

    def stats_for(index):
        return stats_ref.at[:, :, pl.ds(pl.multiple_of(index * row_count, row_count), row_count)]

    own = [
        links.move(weighted_ref.at[seq.me], partials.at[seq.me]),
        links.move(stats_for(seq.me), stats.at[seq.me]),
    ]
    greet([seq.peer(*which) for which in seq.everyone()] + grid.neighbours())
    copies = []
    for which in seq.everyone():
        index = seq.index(*which)
        copies.append(links.send(stats_for(index), stats.at[seq.me], seq.peer(*which)))
        copies.append(links.send(weighted_ref.at[index], partials.at[seq.me], seq.peer(*which)))
    for copy in own:
        copy.wait()
    for copy in copies:
        copy.wait_recv()
    load.wait()
    hidden_load.wait()
    head_count = width // HD
    shares = []
    for h in range(head_count):
        peaks = [stats[d, h, 0:1, :] for d in range(seq_count)]
        top = functools.reduce(jnp.maximum, peaks)
        scales = [jnp.exp(peak - top) for peak in peaks]
        total = sum(scale * stats[d, h, 1:2, :] for d, scale in enumerate(scales))
        shares += [scale / total for scale in scales]
    shares = columns_of(jnp.concatenate(shares))
    for h in range(head_count):
        merged = jnp.zeros((row_count, HD), jnp.float32)
        for d in range(seq_count):
            column = h * seq_count + d
            merged += (
                partials[d, :, h * HD : (h + 1) * HD].astype(jnp.float32)
                * shares[:, column : column + 1]
            )
        attention[seq.me, :, h * HD : (h + 1) * HD] = merged.astype(jnp.bfloat16)
    block_sum = BlockSum(links, grid, seq, parts, from_x, summed, from_z)

    def use(s):
        block_sum.put(
            s, jnp.dot(attention[s], weight[...], preferred_element_type=jnp.float32)
        )

    share_over_seq(links, seq, attention, use)
    for s, total in block_sum.totals():
        squares[0, s] = jnp.broadcast_to(
            jnp.sum(total * total, axis=1, keepdims=True), (part_rows, HD)
        )
        landing[s] = total
    square_copies = []
    for k, which in enumerate(seq.everyone(), 1):
        square_copies.append(links.send(squares.at[0], squares.at[k], seq.peer(*which)))
    for copy in square_copies:
        copy.wait_recv()
    factor = lax.rsqrt(jnp.sum(squares[...], axis=0) / (depth * seq_count) + EPSILON)
    update = landing[...] * factor[:, :, 0:1] * attention_gain[seq.me]
    mixed[grid.z, grid.x] = (hidden[...].astype(jnp.float32) + update).astype(jnp.bfloat16)

    chunks = grid.depth
    order = list(range(1, seq.pairs)) + [0]
    mine = mixed.at[grid.z, grid.x]
    x_copies = {0: [links.send(mine, mine, grid.x_peer(o)) for o in range(1, grid.width)]}
    z_copies = {c: links.send(mine, mine, grid.z_peer(chunks - c)) for c in range(1, chunks)}
    mixed_copies = [
        links.send(mixed.at[grid.z, grid.x, seq.index(*which)], mixed_parts.at[seq.me], peer)
        for which, peer in [(which, seq.peer(*which)) for which in seq.everyone()]
    ]
    mixed_parts[seq.me] = mixed[grid.z, grid.x, seq.me]
    for gate_load in gate_loads:
        gate_load.wait()
    down_load.wait()
    near, far, act_far, act_near, part_copies, sum_copies = {}, {}, {}, {}, {}, {}

    def pass_mixed(c):
        z_copies[c].wait_recv()
        block = mixed.at[grid.along_z(c), grid.x]
        x_copies[c] = [links.send(block, block, grid.x_peer(o)) for o in range(1, grid.width)]

    def multiply_gate_up(c):
        for copy in x_copies[c]:
            copy.wait_recv()
        rows = mixed[grid.along_z(c)].astype(jnp.float32)
        rows = rows.reshape(grid.width * seq_count * part_rows, depth).astype(jnp.bfloat16)
        for k in range(2):
            product = lax.dot_general(
                rows, gate_up[k], (((1,), (1,)), ((), ())), preferred_element_type=jnp.float32
            ).astype(jnp.bfloat16)
            for x in range(grid.width):
                for s in range(seq_count):
                    at = (x * seq_count + s) * part_rows
                    outgoing[c, s, k, x] = product[at : at + part_rows]
        for offset in order:
            near[c, offset] = links.send(
                outgoing.at[c, seq.index(offset, 1)],
                from_sibling.at[c, offset],
                seq.peer(0, 1),
            )

    def sum_of_pair(c, offset):
        near[c, offset].wait_recv()
        return outgoing[c, seq.index(offset, 0)].astype(jnp.float32) + from_sibling[
            c, offset
        ].astype(jnp.float32)

    def send_pair_sums(c):
        for offset in order[:-1]:
            outgoing[c, seq.index(offset, 0)] = sum_of_pair(c, offset).astype(jnp.bfloat16)
            far[c, offset] = links.send(
                outgoing.at[c, seq.index(offset, 0)],
                from_pairs.at[c, offset],
                seq.peer(offset, 0),
            )

    def activate(c):
        total = sum_of_pair(c, 0)
        for offset in order[:-1]:
            far[c, offset].wait_recv()
            total += from_pairs[c, offset].astype(jnp.float32)
        gate, up = total[0], total[1]
        activation[c, seq.me] = (gate / (1.0 + jnp.exp(-gate)) * up).astype(jnp.bfloat16)
        block = activation.at[c, seq.me]
        for offset in order[:-1]:
            act_far[c, offset] = links.send(block, block, seq.peer(offset, 0))
        act_near[c] = [links.send(block, block, seq.peer(0, 1))]

    def pass_activation(c):
        for offset in order[:-1]:
            act_far[c, seq.pairs - offset].wait_recv()
            block = activation.at[c, seq.index(offset, 0)]
            act_near[c].append(links.send(block, block, seq.peer(0, 1)))

    def multiply_down(c):
        for copy in act_near[c]:
            copy.wait_recv()
        rows = activation[c].astype(jnp.float32)
        rows = rows.reshape(seq_count * grid.width * part_rows, rows.shape[-1])
        product = jnp.dot(
            rows.astype(jnp.bfloat16), down[...], preferred_element_type=jnp.float32
        ).astype(jnp.bfloat16)
        for s in range(seq_count):
            for x in range(grid.width):
                at = (s * grid.width + x) * part_rows
                feed_parts[c, x, s] = product[at : at + part_rows]
        part_copies[c] = [
            links.send(
                feed_parts.at[c, grid.along_x(o)], feed_from_x.at[c, o], grid.x_peer(o)
            )
            for o in range(1, grid.width)
        ]

    def sum_over_x(c):
        total = feed_parts[c, grid.x].astype(jnp.float32)
        for o, copy in enumerate(part_copies[c], 1):
            copy.wait_recv()
            total += feed_from_x[c, o].astype(jnp.float32)
        feed_summed[c] = total.astype(jnp.bfloat16)
        if c:
            sum_copies[c] = links.send(feed_summed.at[c], feed_from_z.at[c], grid.z_peer(c))

    for step in range(chunks + 3):
        if step < chunks:
            multiply_gate_up(step)
            if step + 1 < chunks:
                pass_mixed(step + 1)
        if 0 <= step - 2 < chunks:
            pass_activation(step - 2)
        if 0 <= step - 3 < chunks:
            sum_over_x(step - 3)
        if step < chunks:
            send_pair_sums(step)
        if 0 <= step - 1 < chunks:
            activate(step - 1)
        if 0 <= step - 2 < chunks:
            multiply_down(step - 2)
    total = feed_summed[0].astype(jnp.float32)
    for c in range(1, chunks):
        sum_copies[c].wait_recv()
        total += feed_from_z[c].astype(jnp.float32)
    halves[...] = total.astype(jnp.bfloat16)
    final_parts[seq.me] = halves[seq.me]
    final_copies = [
        links.send(halves.at[seq.index(*which)], final_parts.at[seq.me], seq.peer(*which))
        for which in seq.everyone()
    ]
    for copy in mixed_copies + final_copies:
        copy.wait_recv()
    pieces = [final_parts[d].astype(jnp.float32) for d in range(seq_count)]
    squares_total = sum(jnp.sum(piece * piece, axis=1, keepdims=True) for piece in pieces)
    factor = lax.rsqrt(squares_total / (depth * seq_count) + EPSILON)
    for d, piece in enumerate(pieces):
        columns = slice(d * depth, (d + 1) * depth)
        out_ref[:, columns] = (
            mixed_parts[d].astype(jnp.float32) + piece * factor * feed_gain[:, columns]
        ).astype(jnp.bfloat16)
    links.finish()


def finish(weighted, stats, weights, hidden, gains, seq_count, blk_count):
    row_count = weighted.shape[1]
    width, depth = weights[0].shape
    units = weights[1].shape[0]
    part_rows = row_count // blk_count
    pairs = seq_count // 2
    across = grid_width(blk_count)
    chunks = blk_count // across
    bf16, f32 = jnp.bfloat16, jnp.float32
    return pl.pallas_call(
        functools.partial(finish_kernel, seq_count, blk_count),
        out_shape=jax.ShapeDtypeStruct((part_rows, depth * seq_count), bf16),
        in_specs=[ANY] * 7 + [VMEM] * 2,
        out_specs=VMEM,
        scratch_shapes=[
            pltpu.VMEM((seq_count, row_count, width), bf16),
            pltpu.VMEM((seq_count, width // HD, 8, row_count), f32),
            pltpu.VMEM((seq_count, row_count, width), bf16),
            pltpu.VMEM((width, depth), bf16),
            pltpu.VMEM((seq_count, seq_count, part_rows, HD), f32),
            pltpu.VMEM((seq_count, part_rows, depth), f32),
            pltpu.VMEM((seq_count, part_rows, depth), bf16),
        ]
        + block_sum_scratch(seq_count, blk_count, part_rows, depth)
        + [
            pltpu.VMEM((2, units, depth), bf16),
            pltpu.VMEM((units, depth), bf16),
            pltpu.VMEM((chunks, across, seq_count, part_rows, depth), bf16),
            pltpu.VMEM((seq_count, part_rows, depth), bf16),
            pltpu.VMEM((seq_count, part_rows, depth), bf16),
            pltpu.VMEM((seq_count, part_rows, depth), bf16),
            pltpu.VMEM((chunks, seq_count, 2, across, part_rows, units), bf16),
            pltpu.VMEM((chunks, pairs, 2, across, part_rows, units), bf16),
            pltpu.VMEM((chunks, pairs, 2, across, part_rows, units), bf16),
            pltpu.VMEM((chunks, seq_count, across, part_rows, units), bf16),
            pltpu.VMEM((chunks, across, seq_count, part_rows, depth), bf16),
            pltpu.VMEM((chunks, across, seq_count, part_rows, depth), bf16),
            pltpu.VMEM((chunks, seq_count, part_rows, depth), bf16),
            pltpu.VMEM((chunks, seq_count, part_rows, depth), bf16),
        ]
        + semaphores(8 * seq_count + (2 * seq_count + 3) * blk_count),
        compiler_params=params(1, 60),
    )(
        weighted,
        stats,
        *weights,
        hidden.reshape(seq_count, blk_count, part_rows, depth),
        gains[0].reshape(seq_count, 1, depth),
        gains[1].reshape(1, -1),
    )


def attention_kernel(
    query_ref,
    factor_ref,
    old_limit_ref,
    new_limit_ref,
    picked_ref,
    turn_ref,
    old_keys_ref,
    old_values_ref,
    key_rows_ref,
    value_rows_ref,
    keys_ref,
    values_ref,
    weighted_ref,
    stats_ref,
):
    @pl.when(pl.program_id(1) == 0)
    def blend():
        row_count = key_rows_ref.shape[0]
        token = lax.broadcasted_iota(jnp.int32, (PLEN, row_count), 0)
        hit = token == picked_ref[...]
        chosen = jnp.where(hit, 1.0, 0.0)
        replaced = jnp.max(chosen, axis=1, keepdims=True) > 0.5
        chosen = chosen.astype(jnp.bfloat16)
        old = old_keys_ref[...].astype(jnp.float32)
        turned = old * turn_ref[0:1, :] + pltpu.roll(old, HD // 2, 1) * turn_ref[1:2, :]
        new_keys = jnp.dot(chosen, key_rows_ref[...], preferred_element_type=jnp.float32)
        keys_ref[...] = jnp.where(replaced, new_keys, turned).astype(jnp.bfloat16)
        new_values = jnp.dot(chosen, value_rows_ref[...], preferred_element_type=jnp.float32)
        values_ref[...] = jnp.where(
            replaced, new_values, old_values_ref[...].astype(jnp.float32)
        ).astype(jnp.bfloat16)

    factor = factor_ref[...] * HD ** (-0.5)
    query = (query_ref[...].astype(jnp.float32) * factor).astype(jnp.bfloat16)
    contract = (((1,), (1,)), ((), ()))
    old_scores = lax.dot_general(
        query, keys_ref[...], contract, preferred_element_type=jnp.float32
    )
    new_scores = lax.dot_general(
        query, key_rows_ref[...], contract, preferred_element_type=jnp.float32
    )
    old_seen = lax.broadcasted_iota(jnp.int32, old_scores.shape, 1) <= old_limit_ref[...].astype(
        jnp.int32
    )
    new_token = lax.broadcasted_iota(jnp.int32, new_scores.shape, 1) - SEL
    new_seen = (new_token >= 0) & (new_token <= new_limit_ref[...].astype(jnp.int32))
    old_scores = jnp.where(old_seen, old_scores, MASKED_SCORE)
    new_scores = jnp.where(new_seen, new_scores, MASKED_SCORE)
    peak = jnp.maximum(
        jnp.max(old_scores, axis=1, keepdims=True), jnp.max(new_scores, axis=1, keepdims=True)
    )
    old_weights = jnp.exp(old_scores - peak)
    new_weights = jnp.exp(new_scores - peak)
    total = jnp.sum(old_weights, axis=1, keepdims=True) + jnp.sum(
        new_weights, axis=1, keepdims=True
    )
    weighted = jnp.dot(
        old_weights.astype(jnp.bfloat16), values_ref[...], preferred_element_type=jnp.float32
    ) + jnp.dot(
        new_weights.astype(jnp.bfloat16), value_rows_ref[...], preferred_element_type=jnp.float32
    )
    weighted_ref[...] = weighted.astype(jnp.bfloat16)
    lane = lax.broadcasted_iota(jnp.int32, weighted.shape, 1)
    stats = jnp.transpose(jnp.where(lane == 0, peak, total))
    stats_ref[0] = stats[:8, :]


def attend(
    queries, factor, old_limit, new_limit, picked, turn, old_keys, old_values, key_rows, value_rows
):
    total_rows, width = queries.shape
    row_count = key_rows.shape[0]
    head_count = width // HD
    block = min(total_rows, 512)
    by_row = pl.BlockSpec((block, 1), lambda h, i: (i, 0))
    by_head = pl.BlockSpec((PLEN, HD), lambda h, i: (0, h))
    rows_by_head = pl.BlockSpec((row_count, HD), lambda h, i: (0, h))
    tile = pl.BlockSpec((block, HD), lambda h, i: (i, h))
    return pl.pallas_call(
        attention_kernel,
        grid=(head_count, total_rows // block),
        out_shape=[
            jax.ShapeDtypeStruct((PLEN, width), jnp.bfloat16),
            jax.ShapeDtypeStruct((PLEN, width), jnp.bfloat16),
            jax.ShapeDtypeStruct((total_rows, width), jnp.bfloat16),
            jax.ShapeDtypeStruct((head_count, 8, total_rows), jnp.float32),
        ],
        in_specs=[
            tile,
            by_row,
            by_row,
            by_row,
            pl.BlockSpec((1, row_count), lambda h, i: (0, 0)),
            pl.BlockSpec((8, HD), lambda h, i: (0, 0)),
            by_head,
            by_head,
            rows_by_head,
            rows_by_head,
        ],
        out_specs=[
            by_head,
            by_head,
            tile,
            pl.BlockSpec((1, 8, block), lambda h, i: (h, 0, i)),
        ],
        compiler_params=pltpu.CompilerParams(vmem_limit_bytes=60 * 1024 * 1024),
    )(
        queries,
        factor,
        old_limit,
        new_limit,
        picked,
        turn,
        old_keys,
        old_values,
        key_rows,
        value_rows,
    )


def frequencies():
    exponents = np.arange(HD // 2, dtype=np.float64) * (-2.0 / HD)
    return np.tile((ROPE_THETA**exponents).astype(np.float32), 2).reshape(1, HD)


def layout(me, seq_count, order, separators, lengths, chosen, lane):
    requests = seq_count // PPR
    openings = []
    for r in range(requests):
        passed = 0
        for slot in range(PPR):
            passed = passed + separators[r, slot]
            openings.append(passed + slot * PLEN)

    def select(pairs):
        return sum(jnp.where(hit, value, 0) for hit, value in pairs)

    starts, owners, new_starts = [], [], []
    for d in range(seq_count):
        hits = [order[k] == d for k in range(seq_count)]
        starts.append(select(zip(hits, openings)))
        owners.append(select((hit, k // PPR) for k, hit in enumerate(hits)))
        base = openings[(d // PPR) * PPR + PPR - 1] + PLEN
        new_starts.append(base + (d % PPR) * TOKN_DEV)
    here = [me == d for d in range(seq_count)]
    my_start = select(zip(here, starts))
    my_owner = select(zip(here, owners))
    my_new_start = select(zip(here, new_starts))
    my_request = lax.div(me, PPR)
    my_length = select((my_request == r, lengths[r]) for r in range(requests))
    last_live = my_length - 1 - lax.rem(me, PPR) * TOKN_DEV
    rows, my_positions, my_picked = [], 0, 0
    for d in range(seq_count):
        picked = chosen[d : d + 1, :]
        positions = jnp.where(lane < SEL, starts[d] + picked, new_starts[d] + lane - SEL)
        request = jnp.where(lane < SEL, owners[d], d // PPR)
        rows.append(jnp.where(request == my_owner, positions - my_start, -1))
        rows.append(
            jnp.where(
                request == my_request, jnp.minimum(positions - my_new_start, last_live), -1
            )
        )
        my_positions = my_positions + jnp.where(here[d], positions, 0)
        my_picked = my_picked + jnp.where(here[d], picked, 0)
    return rows, my_positions, my_start, my_picked


def shards(
    hidden_states,
    query_weight,
    key_weight,
    value_weight,
    output_weight,
    query_gain,
    key_gain,
    attention_gain,
    gate_weight,
    up_weight,
    down_weight,
    feedforward_gain,
    cached_keys,
    cached_values,
    passage_order,
    separators,
    recompute_index,
    prompt_lengths,
):
    seq_count = lax.axis_size("seq")
    blk_count = lax.axis_size("blk")
    row_count = hidden_states.shape[0]
    local_width = query_weight.shape[1]
    total_rows = row_count * seq_count

    hidden, queries, factors, key_rows, value_rows, old_limit, new_limit, picked, turn = project(
        hidden_states,
        (query_weight, key_weight, value_weight),
        (query_gain, key_gain),
        recompute_index,
        passage_order,
        separators,
        prompt_lengths,
        seq_count,
        blk_count,
    )
    passage_keys, passage_values, weighted, stats = attend(
        queries.reshape(total_rows, local_width),
        factors.reshape(total_rows, 1),
        old_limit.reshape(total_rows, 1),
        new_limit.reshape(total_rows, 1),
        picked,
        turn,
        cached_keys[0],
        cached_values[0],
        key_rows,
        value_rows,
    )
    hidden_out = finish(
        weighted.reshape(seq_count, row_count, local_width),
        stats,
        (output_weight, gate_weight.T, up_weight.T, down_weight),
        hidden,
        (attention_gain, feedforward_gain),
        seq_count,
        blk_count,
    )
    return (hidden_out, passage_keys[None], passage_values[None])


def solution(mesh):
    return jax.shard_map(
        shards,
        mesh=mesh,
        in_specs=(
            P("seq", None),
            P("seq", "blk"),
            P("seq", "blk"),
            P("seq", "blk"),
            P("blk", "seq"),
            P("blk"),
            P("blk"),
            P(),
            P("seq", "blk"),
            P("seq", "blk"),
            P("blk", "seq"),
            P(),
            P("seq", None, "blk"),
            P("seq", None, "blk"),
            P(),
            P(),
            P(),
            P(),
        ),
        out_specs=(P(("seq", "blk"), None), P("seq", None, "blk"), P("seq", None, "blk")),
        check_vma=False,
    )
```

```python
import functools

import jax
import jax.numpy as jnp
import numpy as np
from jax import lax
from jax.experimental import pallas as pl
from jax.experimental.pallas import tpu as pltpu
from jax.sharding import PartitionSpec as P

HD = 128
PLEN = 1024
SEL = 96
PPR = 2
TOKN_DEV = 32

EPSILON = 1e-06
ROPE_THETA = 500000.0
MASKED_SCORE = -1e30
MESH = pl.DeviceIdType.MESH
ANY = pl.BlockSpec(memory_space=pl.ANY)
VMEM = pl.BlockSpec(memory_space=pltpu.VMEM)
SMEM = pl.BlockSpec(memory_space=pltpu.SMEM)


def greet(peers):
    barrier = pltpu.get_barrier_semaphore()
    for peer in peers:
        pl.semaphore_signal(barrier, inc=1, device_id=peer, device_id_type=MESH)
    pl.semaphore_wait(barrier, len(peers))


class Links:
    def __init__(self, send_sems, recv_sems, local_sems):
        self.send_sems, self.recv_sems, self.local_sems = send_sems, recv_sems, local_sems
        self.sent, self.moved = 0, 0
        self.unsent, self.started = [], []

    def send(self, source, target, peer):
        copy = pltpu.make_async_remote_copy(
            src_ref=source,
            dst_ref=target,
            send_sem=self.send_sems.at[self.sent],
            recv_sem=self.recv_sems.at[self.sent],
            device_id=peer,
            device_id_type=MESH,
        )
        copy.start()
        self.sent += 1
        self.unsent.append(copy)
        return copy

    def move(self, source, target):
        copy = pltpu.make_async_copy(source, target, self.local_sems.at[self.moved])
        copy.start()
        self.moved += 1
        return copy

    def finish(self):
        for copy in self.unsent:
            copy.wait_send()


class Pairs:
    def __init__(self, count):
        self.count, self.pairs = count, count // 2
        self.me = lax.axis_index("seq")
        self.pair, self.core = lax.div(self.me, 2), lax.rem(self.me, 2)

    def index(self, offset, other):
        core = 1 - self.core if other else self.core
        return lax.rem(self.pair + offset, self.pairs) * 2 + core

    def peer(self, offset, other):
        return {"seq": self.index(offset, other)}

    def everyone(self):
        return [
            (offset, other)
            for offset in list(range(1, self.pairs)) + [0]
            for other in (1, 0)
            if offset or other
        ]

    def source(self, offset, other):
        return ((self.pairs - offset) % self.pairs, other)


class Grid:
    def __init__(self, count):
        self.width = grid_width(count)
        self.depth = count // self.width
        self.me = lax.axis_index("blk")
        self.z, self.x = lax.div(self.me, self.width), lax.rem(self.me, self.width)

    def along_x(self, offset):
        return lax.rem(self.x + offset, self.width)

    def along_z(self, offset):
        return lax.rem(self.z + offset, self.depth)

    def x_peer(self, offset):
        return {"blk": self.z * self.width + self.along_x(offset)}

    def z_peer(self, offset):
        return {"blk": self.along_z(offset) * self.width + self.x}

    def neighbours(self):
        return [self.x_peer(o) for o in range(1, self.width)] + [
            self.z_peer(o) for o in range(1, self.depth)
        ]


def grid_width(count):
    width = 1
    while 8 * width * width <= count:
        width *= 2
    return width


def reduce_over_seq(links, seq, partial, outgoing, from_sibling, from_pairs):
    near, far = {}, []
    order = list(range(1, seq.pairs)) + [0]
    for offset in order:
        for k, piece in enumerate(partial(offset, 1)):
            outgoing[offset, 0, k] = piece.astype(jnp.bfloat16)
        near[offset] = links.send(
            outgoing.at[offset, 0], from_sibling.at[offset], seq.peer(0, 1)
        )
    for offset in order[:-1]:
        pieces = partial(offset, 0)
        near[offset].wait_recv()
        for k, piece in enumerate(pieces):
            outgoing[offset, 1, k] = (piece + from_sibling[offset, k].astype(jnp.float32)).astype(
                jnp.bfloat16
            )
        far.append(
            links.send(outgoing.at[offset, 1], from_pairs.at[offset], seq.peer(offset, 0))
        )
    totals = list(partial(0, 0))
    near[0].wait_recv()
    totals = [t + from_sibling[0, k].astype(jnp.float32) for k, t in enumerate(totals)]
    for offset, copy in zip(order[:-1], far):
        copy.wait_recv()
        totals = [t + from_pairs[offset, k].astype(jnp.float32) for k, t in enumerate(totals)]
    return totals


def share_over_seq(links, seq, buffer, use):
    mine = buffer.at[seq.me]
    far = {o: links.send(mine, mine, seq.peer(o, 0)) for o in range(1, seq.pairs)}
    near = {0: links.send(mine, mine, seq.peer(0, 1))}
    use(seq.me)
    near[0].wait_recv()
    use(seq.index(0, 1))
    for offset in range(1, seq.pairs):
        far[seq.pairs - offset].wait_recv()
        block = buffer.at[seq.index(offset, 0)]
        near[offset] = links.send(block, block, seq.peer(0, 1))
        use(seq.index(offset, 0))
    for offset in range(1, seq.pairs):
        near[offset].wait_recv()
        use(seq.index(offset, 1))


class BlockSum:
    def __init__(self, links, grid, seq, parts, from_x, summed, from_z):
        self.links, self.grid, self.seq = links, grid, seq
        self.parts, self.from_x, self.summed, self.from_z = parts, from_x, summed, from_z
        self.order, self.x_copies, self.z_copies = [], [], []

    def put(self, s, product):
        grid = self.grid
        rows = self.parts.shape[3]
        for z in range(grid.depth):
            for x in range(grid.width):
                at = (z * grid.width + x) * rows
                self.parts[s, z, x] = product[at : at + rows].astype(jnp.bfloat16)
        step = len(self.order)
        self.order.append(s)
        self.x_copies.append(
            [
                self.links.send(
                    self.parts.at[s, :, grid.along_x(o)],
                    self.from_x.at[o, step],
                    grid.x_peer(o),
                )
                for o in range(1, grid.width)
            ]
        )
        if step:
            self.pass_on(step - 1)

    def pass_on(self, step):
        grid = self.grid
        s = self.order[step]
        total = self.parts[s, :, grid.x].astype(jnp.float32)
        for o, copy in enumerate(self.x_copies[step], 1):
            copy.wait_recv()
            total += self.from_x[o, step].astype(jnp.float32)
        self.summed[step] = total.astype(jnp.bfloat16)
        self.z_copies.append(
            [
                self.links.send(
                    self.summed.at[step, grid.along_z(o)],
                    self.from_z.at[o, step],
                    grid.z_peer(o),
                )
                for o in range(1, grid.depth)
            ]
        )

    def totals(self):
        self.pass_on(len(self.order) - 1)
        for step, s in enumerate(self.order):
            total = self.summed[step, self.grid.z].astype(jnp.float32)
            for o, copy in enumerate(self.z_copies[step], 1):
                copy.wait_recv()
                total += self.from_z[o, step].astype(jnp.float32)
            yield s, total


def block_sum_scratch(seq_count, blk_count, part_rows, depth):
    width = grid_width(blk_count)
    height = blk_count // width
    return [
        pltpu.VMEM((seq_count, height, width, part_rows, depth), jnp.bfloat16),
        pltpu.VMEM((width, seq_count, height, part_rows, depth), jnp.bfloat16),
        pltpu.VMEM((seq_count, height, part_rows, depth), jnp.bfloat16),
        pltpu.VMEM((height, seq_count, part_rows, depth), jnp.bfloat16),
    ]


def semaphores(copies):
    return [
        pltpu.SemaphoreType.DMA((copies,)),
        pltpu.SemaphoreType.DMA((copies,)),
        pltpu.SemaphoreType.DMA((8,)),
    ]


def params(collective_id, mebibytes):
    return pltpu.CompilerParams(
        collective_id=collective_id,
        has_side_effects=True,
        vmem_limit_bytes=mebibytes * 1024 * 1024,
    )


def columns_of(rows):
    lanes = rows.shape[1]
    return jnp.transpose(
        jnp.concatenate([rows, jnp.zeros((lanes - rows.shape[0], lanes), jnp.float32)])
    )


def project_kernel(
    seq_count,
    blk_count,
    states_ref,
    query_weight,
    key_weight,
    value_weight,
    query_gain,
    key_gain,
    frequency_ref,
    recompute_ref,
    order_ref,
    separators_ref,
    lengths_ref,
    hidden_ref,
    queries_ref,
    factors_ref,
    key_rows_ref,
    value_rows_ref,
    old_limit_ref,
    new_limit_ref,
    picked_ref,
    turn_ref,
    outgoing,
    from_sibling,
    from_pairs,
    weights,
    squares,
    landing,
    sums,
    chosen,
    *sems,
):
    seq = Pairs(seq_count)
    row_count, depth = hidden_ref.shape[1:]
    width = key_rows_ref.shape[1]
    links = Links(*sems)
    blk = lax.axis_index("blk")
    blk_peers = [{"blk": lax.rem(blk + o, blk_count)} for o in range(1, blk_count)]
    loads = [
        links.move(ref, weights.at[k])
        for k, ref in enumerate((query_weight, key_weight, value_weight))
    ]
    own = links.move(
        states_ref.at[:, pl.ds(pl.multiple_of(seq.me * depth, depth), depth)],
        hidden_ref.at[seq.me],
    )
    greet([seq.peer(*which) for which in seq.everyone()] + blk_peers)
    arrivals = {}
    for which in seq.everyone():
        column = pl.multiple_of(seq.index(*which) * depth, depth)
        arrivals[which] = links.send(
            states_ref.at[:, pl.ds(column, depth)], hidden_ref.at[seq.me], seq.peer(*which)
        )
    chosen[:, :SEL] = recompute_ref[...]
    lane = lax.broadcasted_iota(jnp.int32, (1, row_count), 1)
    limits, my_positions, my_start, my_picked = layout(
        seq.me, seq_count, order_ref, separators_ref, lengths_ref, chosen, lane
    )
    picked_ref[...] = jnp.where(lane < SEL, my_picked, -1)
    limits = columns_of(jnp.concatenate(limits + [my_positions]).astype(jnp.float32))
    for d in range(seq_count):
        old_limit_ref[d] = limits[:, 2 * d : 2 * d + 1]
        new_limit_ref[d] = limits[:, 2 * d + 1 : 2 * d + 2]
    frequency = frequency_ref[...]
    side = jnp.where(lane < HD // 2, -1.0, 1.0)
    turn_angles = my_start.astype(jnp.float32) * frequency
    turn_ref[0:1, :] = jnp.cos(turn_angles)
    turn_ref[1:2, :] = jnp.sin(turn_angles) * side
    angles = limits[:, 2 * seq_count : 2 * seq_count + 1] * frequency
    cosine, sine = jnp.cos(angles), jnp.sin(angles) * side
    for load in loads:
        load.wait()

    def partial(offset, other):
        if offset or other:
            arrivals[seq.source(offset, other)].wait_recv()
        else:
            own.wait()
        rows = hidden_ref[seq.index(offset, other)]
        return [
            jnp.dot(rows, weights[k], preferred_element_type=jnp.float32) for k in range(3)
        ]

    query, key, value = reduce_over_seq(links, seq, partial, outgoing, from_sibling, from_pairs)
    value_rows_ref[...] = value.astype(jnp.bfloat16)
    lane = lax.broadcasted_iota(jnp.int32, (row_count, HD), 1)
    query_squares = jnp.sum(query * query, axis=1, keepdims=True)
    key_squares = jnp.sum(key * key, axis=1, keepdims=True)
    squares[...] = jnp.transpose(jnp.where(lane == 0, query_squares, key_squares))[:8]
    parts = [
        links.send(squares, landing.at[o], blk_peers[o - 1]) for o in range(1, blk_count)
    ]

    def turned(raw, gain, h):
        piece = raw[:, h * HD : (h + 1) * HD] * gain[:, h * HD : (h + 1) * HD]
        return piece * cosine + pltpu.roll(piece, HD // 2, 1) * sine

    for h in range(width // HD):
        queries_ref[seq.me, :, h * HD : (h + 1) * HD] = turned(query, query_gain, h).astype(
            jnp.bfloat16
        )
    mine = queries_ref.at[seq.me]
    far = {o: links.send(mine, mine, seq.peer(o, 0)) for o in range(1, seq.pairs)}
    near = [links.send(mine, mine, seq.peer(0, 1))]
    total = squares[...]
    for o, copy in enumerate(parts, 1):
        copy.wait_recv()
        total += landing[o]
    sums[seq.me] = total
    sum_copies = [
        links.send(sums.at[seq.me], sums.at[seq.me], seq.peer(*which))
        for which in seq.everyone()
    ]
    key_factor = lax.rsqrt(columns_of(total) / (width * blk_count) + EPSILON)[:, 1:2]
    for h in range(width // HD):
        key_rows_ref[:, h * HD : (h + 1) * HD] = (turned(key, key_gain, h) * key_factor).astype(
            jnp.bfloat16
        )
    for offset in range(1, seq.pairs):
        far[seq.pairs - offset].wait_recv()
        block = queries_ref.at[seq.index(offset, 0)]
        near.append(links.send(block, block, seq.peer(0, 1)))
    for copy in sum_copies + near:
        copy.wait_recv()
    for d in range(seq_count):
        factors_ref[d] = lax.rsqrt(columns_of(sums[d]) / (width * blk_count) + EPSILON)[:, 0:1]
    links.finish()


def project(
    states, weights, gains, recompute_index, passage_order, separators, lengths, seq_count, blk_count
):
    row_count = states.shape[0]
    depth, width = weights[0].shape
    pairs = seq_count // 2
    bf16, f32 = jnp.bfloat16, jnp.float32
    return pl.pallas_call(
        functools.partial(project_kernel, seq_count, blk_count),
        out_shape=[
            jax.ShapeDtypeStruct((seq_count, row_count, depth), bf16),
            jax.ShapeDtypeStruct((seq_count, row_count, width), bf16),
            jax.ShapeDtypeStruct((seq_count, row_count, 1), f32),
            jax.ShapeDtypeStruct((row_count, width), bf16),
            jax.ShapeDtypeStruct((row_count, width), bf16),
            jax.ShapeDtypeStruct((seq_count, row_count, 1), f32),
            jax.ShapeDtypeStruct((seq_count, row_count, 1), f32),
            jax.ShapeDtypeStruct((1, row_count), jnp.int32),
            jax.ShapeDtypeStruct((8, HD), f32),
        ],
        in_specs=[ANY] * 4 + [VMEM] * 4 + [SMEM] * 3,
        out_specs=[VMEM] * 9,
        scratch_shapes=[
            pltpu.VMEM((pairs, 2, 3, row_count, width), bf16),
            pltpu.VMEM((pairs, 3, row_count, width), bf16),
            pltpu.VMEM((pairs, 3, row_count, width), bf16),
            pltpu.VMEM((3, depth, width), bf16),
            pltpu.VMEM((8, row_count), f32),
            pltpu.VMEM((blk_count, 8, row_count), f32),
            pltpu.VMEM((seq_count, 8, row_count), f32),
            pltpu.VMEM((seq_count, row_count), jnp.int32),
        ]
        + semaphores(5 * seq_count + blk_count),
        compiler_params=params(0, 60),
    )(
        states,
        *weights,
        *[g.reshape(1, width) for g in gains],
        frequencies(),
        recompute_index,
        passage_order,
        separators,
        lengths,
    )


def blend(h, picked, turn, old_keys, old_values, key_rows, value_rows, keys, values):
    columns = slice(h * HD, (h + 1) * HD)
    row_count = key_rows.shape[0]
    token = lax.broadcasted_iota(jnp.int32, (PLEN, row_count), 0)
    chosen = jnp.where(token == picked, 1.0, 0.0)
    replaced = jnp.max(chosen, axis=1, keepdims=True) > 0.5
    chosen = chosen.astype(jnp.bfloat16)
    old = old_keys[0, :, columns].astype(jnp.float32)
    turned = old * turn[0:1, :] + pltpu.roll(old, HD // 2, 1) * turn[1:2, :]
    new_keys = jnp.dot(chosen, key_rows[:, columns], preferred_element_type=jnp.float32)
    keys[0, :, columns] = jnp.where(replaced, new_keys, turned).astype(jnp.bfloat16)
    new_values = jnp.dot(chosen, value_rows[:, columns], preferred_element_type=jnp.float32)
    values[0, :, columns] = jnp.where(
        replaced, new_values, old_values[0, :, columns].astype(jnp.float32)
    ).astype(jnp.bfloat16)


def attend(h, query, old_limit, new_limit, keys, values, key_rows, value_rows):
    columns = slice(h * HD, (h + 1) * HD)
    contract = (((1,), (1,)), ((), ()))
    old_scores = lax.dot_general(
        query, keys[0, :, columns], contract, preferred_element_type=jnp.float32
    )
    new_scores = lax.dot_general(
        query, key_rows[:, columns], contract, preferred_element_type=jnp.float32
    )
    old_seen = lax.broadcasted_iota(jnp.int32, old_scores.shape, 1) <= old_limit
    new_token = lax.broadcasted_iota(jnp.int32, new_scores.shape, 1) - SEL
    new_seen = (new_token >= 0) & (new_token <= new_limit)
    old_scores = jnp.where(old_seen, old_scores, MASKED_SCORE)
    new_scores = jnp.where(new_seen, new_scores, MASKED_SCORE)
    peak = jnp.maximum(
        jnp.max(old_scores, axis=1, keepdims=True), jnp.max(new_scores, axis=1, keepdims=True)
    )
    old_weights = jnp.exp(old_scores - peak)
    new_weights = jnp.exp(new_scores - peak)
    total = jnp.sum(old_weights, axis=1, keepdims=True) + jnp.sum(
        new_weights, axis=1, keepdims=True
    )
    weighted = jnp.dot(
        old_weights.astype(jnp.bfloat16),
        values[0, :, columns],
        preferred_element_type=jnp.float32,
    ) + jnp.dot(
        new_weights.astype(jnp.bfloat16),
        value_rows[:, columns],
        preferred_element_type=jnp.float32,
    )
    lane = lax.broadcasted_iota(jnp.int32, weighted.shape, 1)
    return weighted.astype(jnp.bfloat16), jnp.transpose(jnp.where(lane == 0, peak, total))[:8]


def finish_kernel(
    seq_count,
    blk_count,
    weight_ref,
    gate_ref,
    up_ref,
    down_ref,
    hidden_ref,
    old_keys_ref,
    old_values_ref,
    queries_ref,
    factors_ref,
    old_limit_ref,
    new_limit_ref,
    picked_ref,
    turn_ref,
    key_rows_ref,
    value_rows_ref,
    attention_gain,
    feed_gain,
    out_ref,
    keys_ref,
    values_ref,
    old_keys,
    old_values,
    weighted,
    own_stats,
    partials,
    stats,
    attention,
    weight,
    squares,
    landing,
    hidden,
    parts,
    from_x,
    summed,
    from_z,
    gate_up,
    down,
    mixed,
    mixed_parts,
    final_parts,
    halves,
    outgoing,
    from_sibling,
    from_pairs,
    activation,
    feed_parts,
    feed_from_x,
    feed_summed,
    feed_from_z,
    *sems,
):
    seq, grid = Pairs(seq_count), Grid(blk_count)
    row_count, width = attention.shape[1:]
    part_rows, depth = mixed.shape[3:]
    links = Links(*sems)
    cache_loads = [links.move(old_keys_ref, old_keys), links.move(old_values_ref, old_values)]
    load = links.move(weight_ref, weight)
    gate_loads = [links.move(gate_ref, gate_up.at[0]), links.move(up_ref, gate_up.at[1])]
    down_load = links.move(down_ref, down)
    hidden_load = links.move(hidden_ref.at[:, grid.me], hidden)
    greet([seq.peer(*which) for which in seq.everyone()] + grid.neighbours())
    for cache_load in cache_loads:
        cache_load.wait()
    head_count = width // HD
    group = min(seq_count, 4)
    copies = []
    for h in range(head_count):
        columns = slice(h * HD, (h + 1) * HD)
        blend(
            h,
            picked_ref[...],
            turn_ref,
            old_keys,
            old_values,
            key_rows_ref,
            value_rows_ref,
            keys_ref,
            values_ref,
        )
        for first in range(0, seq_count, group):
            some = slice(first, first + group)
            rows = group * row_count
            factor = factors_ref[some].reshape(rows, 1) * HD ** (-0.5)
            query = queries_ref[some, :, columns].reshape(rows, HD).astype(jnp.float32) * factor
            values, tile = attend(
                h,
                query.astype(jnp.bfloat16),
                old_limit_ref[some].reshape(rows, 1).astype(jnp.int32),
                new_limit_ref[some].reshape(rows, 1).astype(jnp.int32),
                keys_ref,
                values_ref,
                key_rows_ref,
                value_rows_ref,
            )
            for d in range(group):
                at = slice(d * row_count, (d + 1) * row_count)
                weighted[h, first + d] = values[at]
                own_stats[h, first + d] = tile[:, at]
        for which in seq.everyone():
            index, peer = seq.index(*which), seq.peer(*which)
            copies.append(links.send(own_stats.at[h, index], stats.at[h, seq.me], peer))
            copies.append(links.send(weighted.at[h, index], partials.at[h, seq.me], peer))
        stats[h, seq.me] = own_stats[h, seq.me]
        partials[h, seq.me] = weighted[h, seq.me]
    for copy in copies:
        copy.wait_recv()
    load.wait()
    hidden_load.wait()
    shares = []
    for h in range(head_count):
        peaks = [stats[h, d, 0:1, :] for d in range(seq_count)]
        top = functools.reduce(jnp.maximum, peaks)
        scales = [jnp.exp(peak - top) for peak in peaks]
        total = sum(scale * stats[h, d, 1:2, :] for d, scale in enumerate(scales))
        shares += [scale / total for scale in scales]
    shares = columns_of(jnp.concatenate(shares))
    for h in range(head_count):
        merged = jnp.zeros((row_count, HD), jnp.float32)
        for d in range(seq_count):
            column = h * seq_count + d
            merged += partials[h, d].astype(jnp.float32) * shares[:, column : column + 1]
        attention[seq.me, :, h * HD : (h + 1) * HD] = merged.astype(jnp.bfloat16)
    block_sum = BlockSum(links, grid, seq, parts, from_x, summed, from_z)

    def use(s):
        block_sum.put(
            s, jnp.dot(attention[s], weight[...], preferred_element_type=jnp.float32)
        )

    share_over_seq(links, seq, attention, use)
    for s, total in block_sum.totals():
        squares[0, s] = jnp.broadcast_to(
            jnp.sum(total * total, axis=1, keepdims=True), (part_rows, HD)
        )
        landing[s] = total
    square_copies = []
    for k, which in enumerate(seq.everyone(), 1):
        square_copies.append(links.send(squares.at[0], squares.at[k], seq.peer(*which)))
    for copy in square_copies:
        copy.wait_recv()
    factor = lax.rsqrt(jnp.sum(squares[...], axis=0) / (depth * seq_count) + EPSILON)
    update = landing[...] * factor[:, :, 0:1] * attention_gain[seq.me]
    mixed[grid.z, grid.x] = (hidden[...].astype(jnp.float32) + update).astype(jnp.bfloat16)

    chunks = grid.depth
    order = list(range(1, seq.pairs)) + [0]
    mine = mixed.at[grid.z, grid.x]
    x_copies = {0: [links.send(mine, mine, grid.x_peer(o)) for o in range(1, grid.width)]}
    z_copies = {c: links.send(mine, mine, grid.z_peer(chunks - c)) for c in range(1, chunks)}
    mixed_copies = [
        links.send(mixed.at[grid.z, grid.x, seq.index(*which)], mixed_parts.at[seq.me], peer)
        for which, peer in [(which, seq.peer(*which)) for which in seq.everyone()]
    ]
    mixed_parts[seq.me] = mixed[grid.z, grid.x, seq.me]
    for gate_load in gate_loads:
        gate_load.wait()
    down_load.wait()
    near, far, act_far, act_near, part_copies, sum_copies = {}, {}, {}, {}, {}, {}

    def pass_mixed(c):
        z_copies[c].wait_recv()
        block = mixed.at[grid.along_z(c), grid.x]
        x_copies[c] = [links.send(block, block, grid.x_peer(o)) for o in range(1, grid.width)]

    def multiply_gate_up(c):
        for copy in x_copies[c]:
            copy.wait_recv()
        rows = mixed[grid.along_z(c)].astype(jnp.float32)
        rows = rows.reshape(grid.width * seq_count * part_rows, depth).astype(jnp.bfloat16)
        for k in range(2):
            product = lax.dot_general(
                rows, gate_up[k], (((1,), (1,)), ((), ())), preferred_element_type=jnp.float32
            ).astype(jnp.bfloat16)
            for x in range(grid.width):
                for s in range(seq_count):
                    at = (x * seq_count + s) * part_rows
                    outgoing[c, s, k, x] = product[at : at + part_rows]
        for offset in order:
            near[c, offset] = links.send(
                outgoing.at[c, seq.index(offset, 1)],
                from_sibling.at[c, offset],
                seq.peer(0, 1),
            )

    def sum_of_pair(c, offset):
        near[c, offset].wait_recv()
        return outgoing[c, seq.index(offset, 0)].astype(jnp.float32) + from_sibling[
            c, offset
        ].astype(jnp.float32)

    def send_pair_sums(c):
        for offset in order[:-1]:
            outgoing[c, seq.index(offset, 0)] = sum_of_pair(c, offset).astype(jnp.bfloat16)
            far[c, offset] = links.send(
                outgoing.at[c, seq.index(offset, 0)],
                from_pairs.at[c, offset],
                seq.peer(offset, 0),
            )

    def activate(c):
        total = sum_of_pair(c, 0)
        for offset in order[:-1]:
            far[c, offset].wait_recv()
            total += from_pairs[c, offset].astype(jnp.float32)
        gate, up = total[0], total[1]
        activation[c, seq.me] = (gate / (1.0 + jnp.exp(-gate)) * up).astype(jnp.bfloat16)
        block = activation.at[c, seq.me]
        for offset in order[:-1]:
            act_far[c, offset] = links.send(block, block, seq.peer(offset, 0))
        act_near[c] = [links.send(block, block, seq.peer(0, 1))]

    def pass_activation(c):
        for offset in order[:-1]:
            act_far[c, seq.pairs - offset].wait_recv()
            block = activation.at[c, seq.index(offset, 0)]
            act_near[c].append(links.send(block, block, seq.peer(0, 1)))

    def multiply_down(c):
        for copy in act_near[c]:
            copy.wait_recv()
        rows = activation[c].astype(jnp.float32)
        rows = rows.reshape(seq_count * grid.width * part_rows, rows.shape[-1])
        product = jnp.dot(
            rows.astype(jnp.bfloat16), down[...], preferred_element_type=jnp.float32
        ).astype(jnp.bfloat16)
        for s in range(seq_count):
            for x in range(grid.width):
                at = (s * grid.width + x) * part_rows
                feed_parts[c, x, s] = product[at : at + part_rows]
        part_copies[c] = [
            links.send(
                feed_parts.at[c, grid.along_x(o)], feed_from_x.at[c, o], grid.x_peer(o)
            )
            for o in range(1, grid.width)
        ]

    def sum_over_x(c):
        total = feed_parts[c, grid.x].astype(jnp.float32)
        for o, copy in enumerate(part_copies[c], 1):
            copy.wait_recv()
            total += feed_from_x[c, o].astype(jnp.float32)
        feed_summed[c] = total.astype(jnp.bfloat16)
        if c:
            sum_copies[c] = links.send(feed_summed.at[c], feed_from_z.at[c], grid.z_peer(c))

    for step in range(chunks + 3):
        if step < chunks:
            multiply_gate_up(step)
            if step + 1 < chunks:
                pass_mixed(step + 1)
        if 0 <= step - 2 < chunks:
            pass_activation(step - 2)
        if 0 <= step - 3 < chunks:
            sum_over_x(step - 3)
        if step < chunks:
            send_pair_sums(step)
        if 0 <= step - 1 < chunks:
            activate(step - 1)
        if 0 <= step - 2 < chunks:
            multiply_down(step - 2)
    total = feed_summed[0].astype(jnp.float32)
    for c in range(1, chunks):
        sum_copies[c].wait_recv()
        total += feed_from_z[c].astype(jnp.float32)
    halves[...] = total.astype(jnp.bfloat16)
    final_parts[seq.me] = halves[seq.me]
    final_copies = [
        links.send(halves.at[seq.index(*which)], final_parts.at[seq.me], seq.peer(*which))
        for which in seq.everyone()
    ]
    for copy in mixed_copies + final_copies:
        copy.wait_recv()
    pieces = [final_parts[d].astype(jnp.float32) for d in range(seq_count)]
    squares_total = sum(jnp.sum(piece * piece, axis=1, keepdims=True) for piece in pieces)
    factor = lax.rsqrt(squares_total / (depth * seq_count) + EPSILON)
    for d, piece in enumerate(pieces):
        columns = slice(d * depth, (d + 1) * depth)
        out_ref[:, columns] = (
            mixed_parts[d].astype(jnp.float32) + piece * factor * feed_gain[:, columns]
        ).astype(jnp.bfloat16)
    links.finish()


def finish(weights, hidden, caches, rows, gains, seq_count, blk_count):
    row_count = hidden.shape[1]
    width, depth = weights[0].shape
    units = weights[1].shape[0]
    part_rows = row_count // blk_count
    pairs = seq_count // 2
    across = grid_width(blk_count)
    chunks = blk_count // across
    bf16, f32 = jnp.bfloat16, jnp.float32
    return pl.pallas_call(
        functools.partial(finish_kernel, seq_count, blk_count),
        out_shape=[
            jax.ShapeDtypeStruct((part_rows, depth * seq_count), bf16),
            jax.ShapeDtypeStruct(caches[0].shape, bf16),
            jax.ShapeDtypeStruct(caches[1].shape, bf16),
        ],
        in_specs=[ANY] * 7 + [VMEM] * 10,
        out_specs=[VMEM] * 3,
        scratch_shapes=[
            pltpu.VMEM(caches[0].shape, bf16),
            pltpu.VMEM(caches[1].shape, bf16),
            pltpu.VMEM((width // HD, seq_count, row_count, HD), bf16),
            pltpu.VMEM((width // HD, seq_count, 8, row_count), f32),
            pltpu.VMEM((width // HD, seq_count, row_count, HD), bf16),
            pltpu.VMEM((width // HD, seq_count, 8, row_count), f32),
            pltpu.VMEM((seq_count, row_count, width), bf16),
            pltpu.VMEM((width, depth), bf16),
            pltpu.VMEM((seq_count, seq_count, part_rows, HD), f32),
            pltpu.VMEM((seq_count, part_rows, depth), f32),
            pltpu.VMEM((seq_count, part_rows, depth), bf16),
        ]
        + block_sum_scratch(seq_count, blk_count, part_rows, depth)
        + [
            pltpu.VMEM((2, units, depth), bf16),
            pltpu.VMEM((units, depth), bf16),
            pltpu.VMEM((chunks, across, seq_count, part_rows, depth), bf16),
            pltpu.VMEM((seq_count, part_rows, depth), bf16),
            pltpu.VMEM((seq_count, part_rows, depth), bf16),
            pltpu.VMEM((seq_count, part_rows, depth), bf16),
            pltpu.VMEM((chunks, seq_count, 2, across, part_rows, units), bf16),
            pltpu.VMEM((chunks, pairs, 2, across, part_rows, units), bf16),
            pltpu.VMEM((chunks, pairs, 2, across, part_rows, units), bf16),
            pltpu.VMEM((chunks, seq_count, across, part_rows, units), bf16),
            pltpu.VMEM((chunks, across, seq_count, part_rows, depth), bf16),
            pltpu.VMEM((chunks, across, seq_count, part_rows, depth), bf16),
            pltpu.VMEM((chunks, seq_count, part_rows, depth), bf16),
            pltpu.VMEM((chunks, seq_count, part_rows, depth), bf16),
        ]
        + semaphores((8 + 2 * width // HD) * seq_count + (2 * seq_count + 3) * blk_count),
        compiler_params=params(1, 60),
    )(
        *weights,
        hidden.reshape(seq_count, blk_count, part_rows, depth),
        *caches,
        *rows,
        gains[0].reshape(seq_count, 1, depth),
        gains[1].reshape(1, -1),
    )


def frequencies():
    exponents = np.arange(HD // 2, dtype=np.float64) * (-2.0 / HD)
    return np.tile((ROPE_THETA**exponents).astype(np.float32), 2).reshape(1, HD)


def layout(me, seq_count, order, separators, lengths, chosen, lane):
    requests = seq_count // PPR
    openings = []
    for r in range(requests):
        passed = 0
        for slot in range(PPR):
            passed = passed + separators[r, slot]
            openings.append(passed + slot * PLEN)

    def select(pairs):
        return sum(jnp.where(hit, value, 0) for hit, value in pairs)

    starts, owners, new_starts = [], [], []
    for d in range(seq_count):
        hits = [order[k] == d for k in range(seq_count)]
        starts.append(select(zip(hits, openings)))
        owners.append(select((hit, k // PPR) for k, hit in enumerate(hits)))
        base = openings[(d // PPR) * PPR + PPR - 1] + PLEN
        new_starts.append(base + (d % PPR) * TOKN_DEV)
    here = [me == d for d in range(seq_count)]
    my_start = select(zip(here, starts))
    my_owner = select(zip(here, owners))
    my_new_start = select(zip(here, new_starts))
    my_request = lax.div(me, PPR)
    my_length = select((my_request == r, lengths[r]) for r in range(requests))
    last_live = my_length - 1 - lax.rem(me, PPR) * TOKN_DEV
    rows, my_positions, my_picked = [], 0, 0
    for d in range(seq_count):
        picked = chosen[d : d + 1, :]
        positions = jnp.where(lane < SEL, starts[d] + picked, new_starts[d] + lane - SEL)
        request = jnp.where(lane < SEL, owners[d], d // PPR)
        rows.append(jnp.where(request == my_owner, positions - my_start, -1))
        rows.append(
            jnp.where(
                request == my_request, jnp.minimum(positions - my_new_start, last_live), -1
            )
        )
        my_positions = my_positions + jnp.where(here[d], positions, 0)
        my_picked = my_picked + jnp.where(here[d], picked, 0)
    return rows, my_positions, my_start, my_picked


def shards(
    hidden_states,
    query_weight,
    key_weight,
    value_weight,
    output_weight,
    query_gain,
    key_gain,
    attention_gain,
    gate_weight,
    up_weight,
    down_weight,
    feedforward_gain,
    cached_keys,
    cached_values,
    passage_order,
    separators,
    recompute_index,
    prompt_lengths,
):
    seq_count = lax.axis_size("seq")
    blk_count = lax.axis_size("blk")
    hidden, queries, factors, key_rows, value_rows, old_limit, new_limit, picked, turn = project(
        hidden_states,
        (query_weight, key_weight, value_weight),
        (query_gain, key_gain),
        recompute_index,
        passage_order,
        separators,
        prompt_lengths,
        seq_count,
        blk_count,
    )
    return finish(
        (output_weight, gate_weight.T, up_weight.T, down_weight),
        hidden,
        (cached_keys, cached_values),
        (queries, factors, old_limit, new_limit, picked, turn, key_rows, value_rows),
        (attention_gain, feedforward_gain),
        seq_count,
        blk_count,
    )


def solution(mesh):
    return jax.shard_map(
        shards,
        mesh=mesh,
        in_specs=(
            P("seq", None),
            P("seq", "blk"),
            P("seq", "blk"),
            P("seq", "blk"),
            P("blk", "seq"),
            P("blk"),
            P("blk"),
            P(),
            P("seq", "blk"),
            P("seq", "blk"),
            P("blk", "seq"),
            P(),
            P("seq", None, "blk"),
            P("seq", None, "blk"),
            P(),
            P(),
            P(),
            P(),
        ),
        out_specs=(P(("seq", "blk"), None), P("seq", None, "blk"), P("seq", None, "blk")),
        check_vma=False,
    )
```
